32 devices in a mesh: blk: 4 (over x, core), uly: 8 (over z, y).
Axes of the slice: x: 2, y: 2, z: 4, core: 2. Of those that a mesh axis runs over, the one named last changes fastest.
Arguments:
- video_tokens: bfloat16 [1536, 3072], P(('blk', 'uly')), may hold values from -6 to 6
- text_tokens: bfloat16 [256, 3072], P('uly'), may hold values from -6 to 6
- video_modulation: bfloat16 [3, 3072], replicated, may hold values from -4 to 4
- text_modulation: bfloat16 [3, 3072], replicated, may hold values from -4 to 4
- video_projection: bfloat16 [3072, 3, 2048], P(None, None, 'uly'), may hold values from -0.109375 to 0.109375
- text_projection: bfloat16 [3072, 3, 2048], P(None, None, 'uly'), may hold values from -0.109375 to 0.109375
- video_output: bfloat16 [2048, 3072], P('uly'), may hold values from -0.125 to 0.125
- text_output: bfloat16 [2048, 3072], P('uly'), may hold values from -0.125 to 0.125
- video_gains: float32 [2, 128], replicated, may hold values from 1 to 12
- text_gains: float32 [2, 128], replicated, may hold values from 1 to 12
Outputs:
- video_attention: bfloat16 [1536, 3072], P(('blk', 'uly'))
- text_attention: bfloat16 [256, 3072], P('uly')
The draws below stay inside these ranges and needn't reach their ends.
All inputs are finite; a program needn't handle non-finite values.
Results may differ from the reference program's by a relative error of at most 0.025.
The reference program's roundings to bfloat16 on the way count: a program that leaves them out, or rounds other values in their place, can miss the bound.
Values may be sent and summed in bfloat16 or wider, within the bound.
No kernel may reach another device: no remote copies, remote signals or barrier semaphores. Data moves between devices by JAX's collectives and lax.ppermute only.
A program may use at most 128 MiB of HBM per device.

```python
import math
import jax
import jax.numpy as jnp
from jax import lax

D = 3072
HD = 128
HEADS = 16
TEXT = 256
VIDEO = 1536
N_ULY = 8


def norm_gains(seed_key):
    baseline_key = jax.random.fold_in(seed_key, 0)
    return jax.random.uniform(baseline_key, (2, HD), jnp.float32, 1.4, 2.6)


def draw_video_gains(key, part):
    return norm_gains(jax.random.fold_in(key, 11))


def draw_text_gains(key, part):
    return norm_gains(jax.random.fold_in(key, 23))


def levels(own_key, extent, cuts, smallest, top_value):
    loudness = 1.0
    for dim, blocks in cuts:
        draws = jax.random.uniform(jax.random.fold_in(jax.random.fold_in(own_key, 6), dim), (blocks,), jnp.float32, smallest / len(cuts), top_value / len(cuts))
        loudness = loudness * jnp.repeat(jnp.exp(draws), extent[dim] // blocks).reshape((-1,) + (1,) * (len(extent) - 1 - dim))
    return loudness


def gaussian(stream_key, dims, scale, most, shards=(), dtype=jnp.bfloat16):
    drawn = jax.random.normal(stream_key, dims, jnp.float32) * scale
    if len(shards) > 0:
        drawn = levels(stream_key, dims, shards, -0.22, 0.18) * drawn
    return jnp.clip(drawn, min=-most, max=most).astype(dtype)


def setup_inputs(seed: int = 0) -> dict:
    splits = jax.random.split(jax.random.key(seed), 11)
    return {
        "video_tokens": gaussian(splits[0], (VIDEO, D), 1.0, 6.0, ((0, 32),)),
        "text_tokens": gaussian(splits[1], (TEXT, D), 1.0, 6.0, ((0, 8),)),
        "video_modulation": gaussian(splits[2], (3, D), 0.8, 4.0),
        "text_modulation": gaussian(splits[3], (3, D), 0.8, 4.0),
        "video_projection": gaussian(splits[4], (D, 3, HEADS * HD), D ** -0.5, 0.109375, ((2, 8),)),
        "text_projection": gaussian(splits[5], (D, 3, HEADS * HD), D ** -0.5, 0.109375, ((2, 8),)),
        "video_output": gaussian(splits[6], (HEADS * HD, D), (HEADS * HD) ** -0.5, 0.125, ((0, 8),)),
        "text_output": gaussian(splits[7], (HEADS * HD, D), (HEADS * HD) ** -0.5, 0.125, ((0, 8),)),
        "video_gains": draw_video_gains(jax.random.fold_in(splits[10], 71), 0),
        "text_gains": draw_text_gains(jax.random.fold_in(splits[10], 71), 0),
    }


EPS_NORM = 1e-06

def modulate(rows, factors):
    floats = rows.astype(jnp.float32)
    centre = floats - lax.optimization_barrier(jnp.mean(floats, axis=-1, keepdims=True))
    spread = lax.optimization_barrier(jnp.mean(centre * centre, axis=-1, keepdims=True))
    normed = centre / jnp.sqrt(spread + EPS_NORM)
    wide = factors.astype(jnp.float32)
    return (normed * (1.0 + wide[1]) + wide[0]).astype(jnp.bfloat16)

def head_norm(vectors, channel_gain):
    inverse = lax.rsqrt(lax.optimization_barrier(jnp.mean(vectors * vectors, axis=-1, keepdims=True)) + EPS_NORM)
    return (vectors * inverse * channel_gain).astype(jnp.bfloat16)

def project(modded, weights, gains):
    mixture = jnp.einsum('td,dch->tch', modded.astype(jnp.float32), weights.astype(jnp.float32))
    row_count = mixture.shape[0]
    per_head = mixture.reshape(row_count, 3, mixture.shape[2] // HD, HD)
    query_rows = head_norm(per_head[:, 0], gains[0])
    key_rows = head_norm(per_head[:, 1], gains[1])
    value_rows = per_head[:, 2].astype(jnp.bfloat16)
    return (query_rows, key_rows, value_rows)

def attend(query_rows, key_rows, value_rows):
    total_rows = query_rows.shape[0]
    step_rows = math.gcd(total_rows, 512)
    query_blocks = query_rows.reshape(total_rows // step_rows, step_rows, query_rows.shape[1], HD)
    keys_wide = key_rows.astype(jnp.float32)
    values_wide = value_rows.astype(jnp.float32)

    def one_block(query_block):
        scores = jnp.einsum('qhd,khd->hqk', query_block.astype(jnp.float32), keys_wide) * HD ** (-0.5)
        highest = lax.optimization_barrier(jnp.max(scores, axis=-1, keepdims=True))
        weights = jnp.exp(scores - highest)
        totals = lax.optimization_barrier(jnp.sum(weights, axis=-1))
        rounded = weights.astype(jnp.bfloat16).astype(jnp.float32)
        mixture = jnp.einsum('hqk,khd->qhd', rounded, values_wide)
        return mixture / jnp.transpose(totals)[:, :, None]
    mixed_out = lax.map(one_block, query_blocks)
    return mixed_out.reshape(total_rows, query_rows.shape[1] * HD).astype(jnp.bfloat16)

def finish(heads_rows, weights, factors):
    group_cols = weights.shape[0] // N_ULY
    summed = jnp.zeros((heads_rows.shape[0], weights.shape[1]), jnp.float32)
    for group in range(N_ULY):
        partial_rows = jnp.dot(heads_rows[:, group * group_cols:(group + 1) * group_cols], weights[group * group_cols:(group + 1) * group_cols], preferred_element_type=jnp.float32)
        rounded = lax.optimization_barrier(partial_rows.astype(jnp.bfloat16))
        summed = summed + rounded.astype(jnp.float32)
    return (summed * factors[2].astype(jnp.float32)).astype(jnp.bfloat16)

def reference(video_tokens, text_tokens, video_modulation, text_modulation, video_projection, text_projection, video_output, text_output, video_gains, text_gains):
    video_query, video_key, video_value = project(modulate(video_tokens, video_modulation), video_projection, video_gains)
    text_query, text_key, text_value = project(modulate(text_tokens, text_modulation), text_projection, text_gains)
    joined_query = jnp.concatenate([video_query, text_query], axis=0)
    joined_key = jnp.concatenate([video_key, text_key], axis=0)
    joined_value = jnp.concatenate([video_value, text_value], axis=0)
    heads_out = attend(joined_query, joined_key, joined_value)
    video_count = video_tokens.shape[0]
    video_attention = finish(heads_out[:video_count], video_output, video_modulation)
    text_attention = finish(heads_out[video_count:], text_output, text_modulation)
    return (video_attention, text_attention)
```

```python
import functools
import math

import jax
import jax.numpy as jnp
from jax import lax
from jax.experimental import pallas as pl
from jax.experimental.pallas import tpu as pltpu
from jax.sharding import PartitionSpec as P

HD = 128
EPS_NORM = 1e-06
F32 = jnp.float32
BF16 = jnp.bfloat16
VMEM = pl.BlockSpec(memory_space=pltpu.VMEM)
SMEM = pl.BlockSpec(memory_space=pltpu.SMEM)


def call(kernel, outs, args, vmem_mib, scratch=(), flops=0, smem=()):
    moved = sum(a.size * a.dtype.itemsize for a in args)
    return pl.pallas_call(
        kernel,
        out_shape=outs,
        in_specs=[SMEM if i in smem else VMEM for i in range(len(args))],
        out_specs=jax.tree.map(lambda _: VMEM, outs),
        scratch_shapes=list(scratch),
        compiler_params=pltpu.CompilerParams(vmem_limit_bytes=vmem_mib << 20),
        cost_estimate=pl.CostEstimate(flops=flops, bytes_accessed=moved, transcendentals=0),
    )(*args)


def ring_routes(axis):
    n = lax.axis_size(axis)
    order = list(range(0, n, 2)) + list(range(1, n, 2))[::-1]
    ahead = [(order[i], order[(i + 1) % n]) for i in range(n)]
    return ahead, [(b, a) for a, b in ahead]


def across(block, distance):
    n = lax.axis_size("blk")
    return lax.ppermute(block, "blk", [(i, i ^ distance) for i in range(n)])


def modulated(rows, factors):
    floats = rows.astype(F32)
    centre = floats - jnp.mean(floats, axis=-1, keepdims=True)
    spread = jnp.mean(centre * centre, axis=-1, keepdims=True)
    wide = factors.astype(F32)
    normed = centre / jnp.sqrt(spread + EPS_NORM)
    return normed * (1.0 + wide[1:2]) + wide[0:1]


def modulate_kernel(part_ref, video_ref, text_ref, vmod_ref, tmod_ref, left_ref, right_ref, text_f32):
    text_rows = left_ref.shape[0] - video_ref.shape[0]
    half = left_ref.shape[1]
    text_f32[...] = text_ref[...].astype(F32)
    start = pl.multiple_of(part_ref[0] * text_rows, text_rows)
    own_text = text_f32[pl.ds(start, text_rows), :]
    video = modulated(video_ref[...], vmod_ref[...])
    text = modulated(own_text, tmod_ref[...])
    both = jnp.concatenate([video, text], axis=0).astype(BF16)
    left_ref[...] = both[:, :half]
    right_ref[...] = both[:, half:]


def head_normed(mixture, gain):
    heads = []
    for h in range(mixture.shape[1] // HD):
        vectors = mixture[:, h * HD : (h + 1) * HD]
        inverse = lax.rsqrt(jnp.mean(vectors * vectors, axis=-1, keepdims=True) + EPS_NORM)
        heads.append(vectors * inverse * gain)
    return jnp.concatenate(heads, axis=1)


def project_kernel(shards, video_rows, *refs):
    chunks = refs[: 2 * shards]
    wv_ref, wt_ref, vgain_ref, tgain_ref, q_ref, kv_ref = refs[2 * shards :]
    width = q_ref.shape[1]
    video, text = [], []
    for side in range(2):
        floats = [chunks[2 * i + side][...].astype(F32) for i in range(shards)]
        video.append(jnp.concatenate([f[:video_rows] for f in floats], axis=0).astype(BF16))
        text.append(jnp.concatenate([f[video_rows:] for f in floats], axis=0).astype(BF16))
    half = video[0].shape[1]

    def mixed(sides, w_ref, j):
        total = jnp.dot(sides[0], w_ref[j, :half, :], preferred_element_type=F32)
        return total + jnp.dot(sides[1], w_ref[j, half:, :], preferred_element_type=F32)

    def joined(j, norm):
        v = mixed(video, wv_ref, j)
        t = mixed(text, wt_ref, j)
        if norm:
            v = head_normed(v, vgain_ref[j : j + 1, :])
            t = head_normed(t, tgain_ref[j : j + 1, :])
        return jnp.concatenate([v, t], axis=0).astype(BF16)

    q_ref[...] = joined(0, True)
    kv_ref[:, :width] = joined(1, True)
    kv_ref[:, width:] = joined(2, False)


def attend_kernel(sizes, video_rows, parts, sources, *refs):
    groups = len(sizes)
    queries = [r[...].astype(F32) for r in refs[:groups]]
    pieces = refs[groups : groups + groups * sources]
    wv_ref, wt_ref = refs[groups + groups * sources : groups + groups * sources + 2]
    outs = refs[groups + groups * sources + 2 :]
    query = jnp.concatenate(queries, axis=0).astype(BF16)
    width = query.shape[1]
    heads = width // HD
    factor = HD ** (-0.5) * math.log2(math.e)
    state = [None] * heads
    for s in range(sources):
        for g in range(groups):
            piece = pieces[s * groups + g]
            rows = piece.shape[0] if s < parts else sizes[g] * video_rows
            for h in range(heads):
                keys = piece[:rows, h * HD : (h + 1) * HD]
                values = piece[:rows, width + h * HD : width + (h + 1) * HD]
                scores = lax.dot_general(
                    keys,
                    query[:, h * HD : (h + 1) * HD],
                    (((1,), (1,)), ((), ())),
                    preferred_element_type=F32,
                )
                highest = jnp.max(scores, axis=0, keepdims=True)
                if state[h] is not None:
                    before, totals, sums = state[h]
                    highest = jnp.maximum(before, highest)
                weights = jnp.exp2((scores - highest) * factor)
                total = jnp.sum(weights, axis=0, keepdims=True)
                mixed = lax.dot_general(
                    values,
                    weights.astype(BF16),
                    (((0,), (0,)), ((), ())),
                    preferred_element_type=F32,
                )
                if state[h] is not None:
                    shrink = jnp.exp2((before - highest) * factor)
                    total = totals * shrink + total
                    mixed = sums * shrink + mixed
                state[h] = (highest, total, mixed)
    flat = jnp.concatenate([sums / totals for _, totals, sums in state], axis=0)
    rows_out = jnp.transpose(flat)
    text_rows = outs[0].shape[0] - video_rows
    video, text = [], []
    start = 0
    for size in sizes:
        video.append(rows_out[start : start + size * video_rows])
        start += size * video_rows
        text.append(rows_out[start : start + size * text_rows])
        start += size * text_rows
    video = jnp.concatenate(video, axis=0).astype(BF16)
    text = jnp.concatenate(text, axis=0).astype(BF16)
    half = outs[0].shape[1]
    for side in range(2):
        columns = slice(side * half, (side + 1) * half)
        yv = jnp.dot(video, wv_ref[:, columns], preferred_element_type=F32)
        yt = jnp.dot(text, wt_ref[:, columns], preferred_element_type=F32)
        for i in range(len(outs) // 2):
            part = [yv[i * video_rows : (i + 1) * video_rows], yt[i * text_rows : (i + 1) * text_rows]]
            outs[2 * i + side][...] = jnp.concatenate(part, axis=0).astype(BF16)


def close_kernel(a0, a1, a2, b0, b1, b2, vmod_ref, tmod_ref, video_ref, text_ref):
    video_rows = video_ref.shape[0]
    half = a0.shape[1]
    for side, refs in enumerate(((a0, a1, a2), (b0, b1, b2))):
        columns = slice(side * half, (side + 1) * half)
        total = refs[0][...].astype(F32) + refs[1][...].astype(F32) + refs[2][...].astype(F32)
        vgate = vmod_ref[2:3, columns].astype(F32)
        tgate = tmod_ref[2:3, columns].astype(F32)
        video_ref[:, columns] = (total[:video_rows] * vgate).astype(BF16)
        text_ref[:, columns] = (total[video_rows:] * tgate).astype(BF16)


def place_kernel(part_ref, *refs):
    pieces, out_ref, wide = refs[:-2], refs[-2], refs[-1]
    rows = pieces[0].shape[0]
    for d, piece in enumerate(pieces):
        start = pl.multiple_of((part_ref[0] ^ d) * rows, rows)
        wide[pl.ds(start, rows), :] = piece[...].astype(F32)
    out_ref[...] = wide[...].astype(BF16)


def local(
    video_tokens,
    text_tokens,
    video_modulation,
    text_modulation,
    video_projection,
    text_projection,
    video_output,
    text_output,
    video_gains,
    text_gains,
):
    n_blk, n_uly = lax.axis_size("blk"), lax.axis_size("uly")
    reach = n_uly // 2
    ahead, back = ring_routes("uly")
    video_rows, width = video_tokens.shape
    half = width // 2
    parts = math.gcd(n_blk, text_tokens.shape[0] // 8)
    text_rows = text_tokens.shape[0] // parts
    shard_rows = video_rows + text_rows
    cols = video_output.shape[0]
    part = lax.rem(lax.axis_index("blk"), parts).reshape(1).astype(jnp.int32)

    chunk = jax.ShapeDtypeStruct((shard_rows, half), BF16)
    own = call(
        modulate_kernel,
        [chunk, chunk],
        (part, video_tokens, text_tokens, video_modulation, text_modulation),
        8,
        [pltpu.VMEM(text_tokens.shape, F32)],
        smem=(0,),
    )

    fa, fb = own
    ba, bb = own
    arrived = []
    for step in range(1, reach + 1):
        fa = lax.ppermute(fa, "uly", ahead)
        bb = lax.ppermute(bb, "uly", back)
        if step < reach:
            fb = lax.ppermute(fb, "uly", ahead)
            ba = lax.ppermute(ba, "uly", back)
            arrived.append([(-step, fa, fb), (step, ba, bb)])
        else:
            arrived.append([(reach, fa, bb)])
    groups = [[(0, *own)]]
    for step in range(reach - 2):
        groups[0] += arrived[step]
    groups += arrived[reach - 2 :]

    wv = jnp.transpose(video_projection, (1, 0, 2))
    wt = jnp.transpose(text_projection, (1, 0, 2))
    queries, pieces = [], []
    for group in groups:
        rows = len(group) * shard_rows
        q, kv = call(
            functools.partial(project_kernel, len(group), video_rows),
            [
                jax.ShapeDtypeStruct((rows, cols), BF16),
                jax.ShapeDtypeStruct((rows, 2 * cols), BF16),
            ],
            [c for _, *pair in group for c in pair] + [wv, wt, video_gains, text_gains],
            32,
            flops=2 * rows * width * 3 * cols,
        )
        queries.append(q)
        pieces.append([kv] + [across(kv, d) for d in range(1, n_blk)])

    slots = [r for group in groups for r, *_ in group]
    partial = call(
        functools.partial(attend_kernel, [len(g) for g in groups], video_rows, parts, n_blk),
        [chunk] * (2 * n_uly),
        queries
        + [pieces[g][d] for d in range(n_blk) for g in range(len(groups))]
        + [video_output, text_output],
        48,
        flops=4 * (shard_rows * n_uly) ** 2 * n_blk * cols,
    )
    mine = {r: (partial[2 * i], partial[2 * i + 1]) for i, r in enumerate(slots)}
    mine[-reach] = mine[reach]

    def joined(arriving, own_part):
        return (arriving.astype(F32) + own_part.astype(F32)).astype(BF16)

    fa, bb = mine[reach][0], mine[-reach][1]
    fb, ba = mine[reach - 1][1], mine[1 - reach][0]
    for left in range(reach - 1, -1, -1):
        fa = lax.ppermute(fa, "uly", ahead)
        bb = lax.ppermute(bb, "uly", back)
        if left:
            fa = joined(fa, mine[left][0])
            bb = joined(bb, mine[-left][1])
            fb = lax.ppermute(fb, "uly", ahead)
            ba = lax.ppermute(ba, "uly", back)
            if left > 1:
                fb = joined(fb, mine[left - 1][1])
                ba = joined(ba, mine[1 - left][0])
    video_attention, text_part = call(
        close_kernel,
        [
            jax.ShapeDtypeStruct(video_tokens.shape, BF16),
            jax.ShapeDtypeStruct((text_rows, width), BF16),
        ],
        (fa, ba, mine[0][0], fb, bb, mine[0][1], video_modulation, text_modulation),
        8,
    )
    text_attention = call(
        place_kernel,
        jax.ShapeDtypeStruct(text_tokens.shape, BF16),
        [part, text_part] + [across(text_part, d) for d in range(1, parts)],
        8,
        [pltpu.VMEM(text_tokens.shape, F32)],
        smem=(0,),
    )
    return (video_attention, text_attention)


def solution(mesh):
    placed = (
        P(("blk", "uly"), None),
        P("uly", None),
        P(),
        P(),
        P(None, None, "uly"),
        P(None, None, "uly"),
        P("uly", None),
        P("uly", None),
        P(),
        P(),
    )
    return jax.shard_map(
        local,
        mesh=mesh,
        in_specs=placed,
        out_specs=(P(("blk", "uly"), None), P("uly", None)),
        check_vma=False,
    )
```

```python
import functools
import math

import jax
import jax.numpy as jnp
from jax import lax
from jax.experimental import pallas as pl
from jax.experimental.pallas import tpu as pltpu
from jax.sharding import PartitionSpec as P

HD = 128
EPS_NORM = 1e-06
F32 = jnp.float32
BF16 = jnp.bfloat16
VMEM = pl.BlockSpec(memory_space=pltpu.VMEM)
HBM = pl.BlockSpec(memory_space=pltpu.HBM)
SMEM = pl.BlockSpec(memory_space=pltpu.SMEM)


def call(kernel, outs, args, vmem_mib, scratch=(), flops=0, smem=(), hbm=()):
    moved = sum(a.size * a.dtype.itemsize for a in args)
    args = [pltpu.with_memory_space_constraint(a, pltpu.HBM) if i in hbm else a for i, a in enumerate(args)]
    return pl.pallas_call(
        kernel,
        out_shape=outs,
        in_specs=[SMEM if i in smem else HBM if i in hbm else VMEM for i in range(len(args))],
        out_specs=jax.tree.map(lambda _: VMEM, outs),
        scratch_shapes=list(scratch),
        compiler_params=pltpu.CompilerParams(vmem_limit_bytes=vmem_mib << 20),
        cost_estimate=pl.CostEstimate(flops=flops, bytes_accessed=moved, transcendentals=0),
    )(*args)


def ring_routes(axis):
    n = lax.axis_size(axis)
    order = list(range(0, n, 2)) + list(range(1, n, 2))[::-1]
    ahead = [(order[i], order[(i + 1) % n]) for i in range(n)]
    across_ring = [(order[i], order[(i + n // 2) % n]) for i in range(n)]
    return ahead, [(b, a) for a, b in ahead], across_ring


def across(block, distance):
    n = lax.axis_size("blk")
    return lax.ppermute(block, "blk", [(i, i ^ distance) for i in range(n)])


def tied(block, *others):
    return lax.optimization_barrier((block, *others))[0]


def modulated(rows, factors):
    floats = rows.astype(F32)
    centre = floats - jnp.mean(floats, axis=-1, keepdims=True)
    spread = jnp.mean(centre * centre, axis=-1, keepdims=True)
    wide = factors.astype(F32)
    normed = centre / jnp.sqrt(spread + EPS_NORM)
    return normed * (1.0 + wide[1:2]) + wide[0:1]


def modulate_kernel(part_ref, *refs):
    sources, (left_ref, right_ref), landed = refs[:4], refs[4:6], refs[6:10]
    text_f32, sems = refs[10:]
    copies = [pltpu.make_async_copy(s, d, sems.at[i]) for i, (s, d) in enumerate(zip(sources, landed))]
    for copy in copies:
        copy.start()
    for copy in copies:
        copy.wait()
    video_ref, text_ref, vmod_ref, tmod_ref = landed
    text_rows = left_ref.shape[0] - video_ref.shape[0]
    half = left_ref.shape[1]
    text_f32[...] = text_ref[...].astype(F32)
    start = pl.multiple_of(part_ref[0] * text_rows, text_rows)
    own_text = text_f32[pl.ds(start, text_rows), :]
    video = modulated(video_ref[...], vmod_ref[...])
    text = modulated(own_text, tmod_ref[...])
    both = jnp.concatenate([video, text], axis=0).astype(BF16)
    left_ref[...] = both[:, :half]
    right_ref[...] = both[:, half:]


def fetch_kernel(count, *refs):
    many = (len(refs) - 1) // 2
    sources, landed, sems = refs[:many], refs[many : 2 * many], refs[-1]
    if count:
        step = sources[0].shape[1] // count
        sources = [s.at[:, i * step : (i + 1) * step, :] for s in sources for i in range(count)]
        landed = [s.at[:, i * step : (i + 1) * step, :] for s in landed for i in range(count)]
    copies = [pltpu.make_async_copy(s, d, sems.at[i]) for i, (s, d) in enumerate(zip(sources, landed))]
    for copy in copies:
        copy.start()
    for copy in copies:
        copy.wait()


def head_normed(mixture, gain):
    heads = []
    for h in range(mixture.shape[1] // HD):
        vectors = mixture[:, h * HD : (h + 1) * HD]
        inverse = lax.rsqrt(jnp.mean(vectors * vectors, axis=-1, keepdims=True) + EPS_NORM)
        heads.append(vectors * inverse * gain)
    return jnp.concatenate(heads, axis=1)


def project_kernel(shards, video_rows, *refs):
    chunks = refs[: 2 * shards]
    wv_ref, wt_ref, vgain_ref, tgain_ref, q_ref, kv_ref = refs[2 * shards :]
    width = q_ref.shape[1]
    video, text = [], []
    for side in range(2):
        floats = [chunks[2 * i + side][...].astype(F32) for i in range(shards)]
        video.append(jnp.concatenate([f[:video_rows] for f in floats], axis=0).astype(BF16))
        text.append(jnp.concatenate([f[video_rows:] for f in floats], axis=0).astype(BF16))
    half = video[0].shape[1]

    def mixed(sides, w_ref, j):
        total = jnp.dot(sides[0], w_ref[j, :half, :], preferred_element_type=F32)
        return total + jnp.dot(sides[1], w_ref[j, half:, :], preferred_element_type=F32)

    def joined(j, norm):
        v = mixed(video, wv_ref, j)
        t = mixed(text, wt_ref, j)
        if norm:
            v = head_normed(v, vgain_ref[j : j + 1, :])
            t = head_normed(t, tgain_ref[j : j + 1, :])
        return jnp.concatenate([v, t], axis=0).astype(BF16)

    q_ref[...] = joined(0, True)
    kv_ref[:, :width] = joined(1, True)
    kv_ref[:, width:] = joined(2, False)


def wide_rows(refs, counts):
    return jnp.concatenate([r[...].astype(F32)[:n] for r, n in zip(refs, counts)], axis=0).astype(BF16)


def absorbed(state, query, block):
    width = query.shape[1]
    factor = HD ** (-0.5) * math.log2(math.e)
    raised = []
    for h in range(width // HD):
        mine = slice(h * HD, (h + 1) * HD)
        scores = lax.dot_general(
            block[:, mine], query[:, mine], (((1,), (1,)), ((), ())), preferred_element_type=F32
        )
        highest = jnp.max(scores, axis=0, keepdims=True)
        if state:
            before, totals, sums = state[h]
            highest = jnp.maximum(before, highest)
        weights = jnp.exp2((scores - highest) * factor)
        total = jnp.sum(weights, axis=0, keepdims=True)
        mixed = lax.dot_general(
            block[:, width + h * HD : width + (h + 1) * HD],
            weights.astype(BF16),
            (((0,), (0,)), ((), ())),
            preferred_element_type=F32,
        )
        if state:
            shrink = jnp.exp2((before - highest) * factor)
            total = totals * shrink + total
            mixed = sums * shrink + mixed
        raised.append((highest, total, mixed))
    return raised


def load_state(stats_ref, sums_ref):
    heads = stats_ref.shape[0] // 2
    return [
        (
            stats_ref[h : h + 1, :],
            stats_ref[heads + h : heads + h + 1, :],
            sums_ref[h * HD : (h + 1) * HD, :],
        )
        for h in range(heads)
    ]


def attend_kernel(sizes, video_rows, with_text, fresh, queries, *refs):
    groups, sources = len(sizes), len(with_text)
    query = wide_rows(refs[:queries], [r.shape[0] for r in refs[:queries]])
    refs = refs[queries:]
    state = []
    if not fresh:
        state = load_state(*refs[:2])
        refs = refs[2:]
    pieces, outs = refs[: groups * sources], refs[groups * sources :]
    if fresh:
        outs[0][...] = query
    stats_ref, sums_ref = outs[-2:]
    for s in range(sources):
        held = pieces[s * groups : (s + 1) * groups]
        counts = [p.shape[0] if with_text[s] else n * video_rows for p, n in zip(held, sizes)]
        state = absorbed(state, query, wide_rows(held, counts))
    heads = len(state)
    for h, (highest, totals, sums) in enumerate(state):
        stats_ref[h : h + 1, :] = highest
        stats_ref[heads + h : heads + h + 1, :] = totals
        sums_ref[h * HD : (h + 1) * HD, :] = sums


def finish_kernel(sizes, video_rows, with_text, query_ref, stats_ref, sums_ref, *refs):
    sources = len(with_text)
    pieces, weights = refs[:sources], refs[sources : sources + 2]
    outs = refs[sources + 2 :]
    counts = [p.shape[0] if w else sizes[-1] * video_rows for p, w in zip(pieces, with_text)]
    state = absorbed(load_state(stats_ref, sums_ref), query_ref[...], wide_rows(pieces, counts))
    flat = jnp.concatenate([sums / totals for _, totals, sums in state], axis=0)
    rows_out = jnp.transpose(flat)
    text_rows = rows_out.shape[0] // sum(sizes) - video_rows
    video, text = [], []
    start = 0
    for size in sizes:
        video.append(rows_out[start : start + size * video_rows])
        start += size * video_rows
        text.append(rows_out[start : start + size * text_rows])
        start += size * text_rows
    shards = [jnp.concatenate(rows, axis=0).astype(BF16) for rows in (video, text)]
    put_partials([0] * sum(sizes), outs, shards, weights)


def rest_kernel(sides, video_ref, text_ref, wv_ref, wt_ref, *outs):
    put_partials(sides, outs, [video_ref[...], text_ref[...]], [wv_ref, wt_ref])


def put_partials(sides, outs, heads, weights):
    outs = list(outs)
    half = outs[0].shape[1]
    counts = [h.shape[0] // len(sides) for h in heads]
    mixed = [
        [jnp.dot(h, w[:, s * half : (s + 1) * half], preferred_element_type=F32) for s in range(2)]
        for h, w in zip(heads, weights)
    ]
    for i, side in enumerate(sides):
        parts = [[y[i * n : (i + 1) * n] for y in ys] for n, ys in zip(counts, mixed)]
        rows = [[y] for y in parts[0]]
        if side is None:
            rows.append(parts[1])
        else:
            rows[side] += parts[1]
        for row in rows:
            outs.pop(0)[...] = jnp.concatenate(row, axis=0).astype(BF16)


def text_side(r, n):
    return 0


def close_text_kernel(fa_ref, ba_ref, own_ref, tmod_ref, text_ref):
    text_rows = text_ref.shape[0]
    half = own_ref.shape[1]
    video_rows = own_ref.shape[0] - 2 * text_rows
    total = sum(r[...].astype(F32)[video_rows:] for r in (fa_ref, ba_ref, own_ref))
    for side in range(2):
        columns = slice(side * half, (side + 1) * half)
        gate = tmod_ref[2:3, columns].astype(F32)
        text_ref[:, columns] = (total[side * text_rows : (side + 1) * text_rows] * gate).astype(BF16)


def close_kernel(part_ref, fa, ba, own_a, fb, bb, own_b, vmod_ref, *refs):
    pieces, (video_ref, text_ref, wide) = refs[:-3], refs[-3:]
    video_rows = video_ref.shape[0]
    half = own_a.shape[1]
    for side, arrivals in enumerate(((fa, ba, own_a), (fb, bb, own_b))):
        columns = slice(side * half, (side + 1) * half)
        total = sum(r[...].astype(F32)[:video_rows] for r in arrivals)
        video_ref[:, columns] = (total * vmod_ref[2:3, columns].astype(F32)).astype(BF16)
    rows = pieces[0].shape[0]
    for d, piece in enumerate(pieces):
        start = pl.multiple_of((part_ref[0] ^ d) * rows, rows)
        wide[pl.ds(start, rows), :] = piece[...].astype(F32)
    text_ref[...] = wide[...].astype(BF16)


def local(
    video_tokens,
    text_tokens,
    video_modulation,
    text_modulation,
    video_projection,
    text_projection,
    video_output,
    text_output,
    video_gains,
    text_gains,
):
    n_blk, n_uly = lax.axis_size("blk"), lax.axis_size("uly")
    reach = n_uly // 2
    ahead, back, opposite = ring_routes("uly")
    video_rows, width = video_tokens.shape
    half = width // 2
    parts = math.gcd(n_blk, text_tokens.shape[0] // 8)
    text_rows = text_tokens.shape[0] // parts
    shard_rows = video_rows + text_rows
    cols = video_output.shape[0]
    part = lax.rem(lax.axis_index("blk"), parts).reshape(1).astype(jnp.int32)

    chunk = jax.ShapeDtypeStruct((shard_rows, half), BF16)
    own = call(
        modulate_kernel,
        [chunk, chunk],
        (part, video_tokens, text_tokens, video_modulation, text_modulation),
        8,
        [pltpu.VMEM(a.shape, BF16) for a in (video_tokens, text_tokens, video_modulation, text_modulation)]
        + [pltpu.VMEM(text_tokens.shape, F32), pltpu.SemaphoreType.DMA((4,))],
        smem=(0,),
        hbm=(1, 2, 3, 4),
    )

    def fetched(arrays, after, count=0):
        arrays = [tied(arrays[0], after), *arrays[1:]]
        return call(
            functools.partial(fetch_kernel, count),
            [jax.ShapeDtypeStruct(a.shape, a.dtype) for a in arrays],
            arrays,
            1,
            [pltpu.SemaphoreType.DMA((len(arrays) * max(count, 1),))],
            hbm=range(len(arrays)),
        )

    weights = [jnp.transpose(p, (1, 0, 2)) for p in (video_projection, text_projection)]
    held, ends, waiting = [], [], []
    queries, pieces, groups = [], [], []

    def fetch_all(after):
        held.extend(fetched(weights, after, 4))
        return held[-1]

    def fetch_rest(after):
        ends.extend(fetched([video_output, text_output, video_gains, text_gains], after))
        return ends[0]

    def project(after, direct=False):
        group = list(waiting)
        waiting.clear()
        rows = len(group) * shard_rows
        chunks = [c for _, *pair in group for c in pair]
        q, kv = call(
            functools.partial(project_kernel, len(group), video_rows),
            [
                jax.ShapeDtypeStruct((rows, cols), BF16),
                jax.ShapeDtypeStruct((rows, 2 * cols), BF16),
            ],
            [tied(chunks[0], after), *chunks[1:], *held, *ends[2:]],
            12,
            flops=2 * rows * width * 3 * cols,
        )
        if direct:
            spread = [kv] + [across(kv, d) for d in range(1, n_blk)]
        else:
            spread = {d: across(kv, d) if d else kv for d in (0, 1, *range(2, n_blk, 2))}
        queries.append(q)
        pieces.append(spread)
        groups.append(group)
        return q

    beside = {(1, 1): [fetch_all], (2, 0): [fetch_rest], (2, 1): [project], (3, 1): [project], (4, 1): [project]}
    fa, fb = own
    ba, bb = own
    waiting.append((0, *own))
    due = []
    for step in range(1, reach + 1):
        behind = fa
        fa = lax.ppermute(tied(fa, *due) if due else fa, "uly", ahead)
        bb = lax.ppermute(bb, "uly", back)
        due = [task(behind) for task in beside.get((step, 0), [])]
        if step < reach:
            behind = fb
            fb = lax.ppermute(tied(fb, *due) if due else fb, "uly", ahead)
            ba = lax.ppermute(ba, "uly", back)
            due = [task(behind) for task in beside.get((step, 1), [])]
            waiting += [(-step, fa, fb), (step, ba, bb)]
        else:
            due = [task(fb) for task in beside.get((step, 1), [])]
            waiting += [(reach, fa, bb)]
            project(fa, True)

    for spread in pieces[:-1]:
        for d in range(3, n_blk, 2):
            spread[d] = across(tied(spread[d - 1], queries[-1]), 1)

    sizes = [len(g) for g in groups]
    slots = [r for group in groups for r, *_ in group]
    total_rows = shard_rows * n_uly
    with_text = [d < parts for d in range(n_blk)]
    state = [
        jax.ShapeDtypeStruct((2 * cols // HD, total_rows), F32),
        jax.ShapeDtypeStruct((cols, total_rows), F32),
    ]
    query, *carried = call(
        functools.partial(attend_kernel, sizes[:-1], video_rows, with_text[:2], True, len(queries)),
        [jax.ShapeDtypeStruct((total_rows, cols), BF16), *state],
        queries + [spread[d] for d in range(2) for spread in pieces[:-1]],
        16,
        flops=8 * total_rows * (total_rows - shard_rows) * cols,
    )
    carried = call(
        functools.partial(attend_kernel, sizes[:-1], video_rows, with_text[2:], False, 1),
        state,
        [query, *carried] + [spread[d] for d in range(2, n_blk) for spread in pieces[:-1]],
        16,
        flops=4 * total_rows * (total_rows - shard_rows) * (n_blk - 2) * cols,
    )
    sides = [text_side(r, n_uly) for r in slots]
    shapes = []
    for side in sides:
        rows = [video_rows, video_rows] + ([2 * text_rows] if side is None else [])
        if side is not None:
            rows[side] += 2 * text_rows
        shapes.append([jax.ShapeDtypeStruct((n, half), BF16) for n in rows])
    partial = call(
        functools.partial(finish_kernel, sizes, video_rows, with_text),
        [shape for group in shapes for shape in group],
        [query, *carried] + pieces[-1] + ends[:2],
        16,
        flops=2 * total_rows * cols * width,
    )
    mine = {}
    for r, group in zip(slots, shapes):
        mine[r], partial = partial[: len(group)], partial[len(group) :]
    mine[-reach] = mine[reach]

    def joined(arriving, own_part):
        return (arriving.astype(F32) + own_part.astype(F32)).astype(BF16)

    fa, bb = mine[reach][0], mine[-reach][1]
    fb, ba = mine[reach - 1][1], mine[1 - reach][0]
    for left in range(reach - 1, -1, -1):
        fa = lax.ppermute(fa, "uly", ahead)
        bb = lax.ppermute(bb, "uly", back)
        if left:
            fa = joined(fa, mine[left][0])
            bb = joined(bb, mine[-left][1])
            fb = lax.ppermute(fb, "uly", ahead)
            ba = lax.ppermute(ba, "uly", back)
            if left > 1:
                fb = joined(fb, mine[left - 1][1])
                ba = joined(ba, mine[1 - left][0])
    text_part = call(
        close_text_kernel,
        jax.ShapeDtypeStruct((text_rows, width), BF16),
        (fa, ba, mine[0][0], text_modulation),
        4,
    )
    pieces = [text_part] + [across(text_part, d) for d in range(1, parts)]
    return tuple(
        call(
            close_kernel,
            [jax.ShapeDtypeStruct(t.shape, BF16) for t in (video_tokens, text_tokens)],
            (part, fa, ba, mine[0][0], fb, bb, mine[0][1], video_modulation, *pieces),
            8,
            [pltpu.VMEM(text_tokens.shape, F32)],
            smem=(0,),
        )
    )


def solution(mesh):
    placed = (
        P(("blk", "uly"), None),
        P("uly", None),
        P(),
        P(),
        P(None, None, "uly"),
        P(None, None, "uly"),
        P("uly", None),
        P("uly", None),
        P(),
        P(),
    )
    return jax.shard_map(
        local,
        mesh=mesh,
        in_specs=placed,
        out_specs=(P(("blk", "uly"), None), P("uly", None)),
        check_vma=False,
    )
```

```python
import functools
import math

import jax
import jax.numpy as jnp
from jax import lax
from jax.experimental import pallas as pl
from jax.experimental.pallas import tpu as pltpu
from jax.sharding import PartitionSpec as P

HD = 128
EPS_NORM = 1e-06
F32 = jnp.float32
BF16 = jnp.bfloat16
VMEM = pl.BlockSpec(memory_space=pltpu.VMEM)
HBM = pl.BlockSpec(memory_space=pltpu.HBM)
SMEM = pl.BlockSpec(memory_space=pltpu.SMEM)


def call(kernel, outs, args, vmem_mib, scratch=(), flops=0, smem=(), hbm=()):
    moved = sum(a.size * a.dtype.itemsize for a in args)
    args = [pltpu.with_memory_space_constraint(a, pltpu.HBM) if i in hbm else a for i, a in enumerate(args)]
    return pl.pallas_call(
        kernel,
        out_shape=outs,
        in_specs=[SMEM if i in smem else HBM if i in hbm else VMEM for i in range(len(args))],
        out_specs=jax.tree.map(lambda _: VMEM, outs),
        scratch_shapes=list(scratch),
        compiler_params=pltpu.CompilerParams(vmem_limit_bytes=vmem_mib << 20),
        cost_estimate=pl.CostEstimate(flops=flops, bytes_accessed=moved, transcendentals=0),
    )(*args)


def ring_routes(axis):
    n = lax.axis_size(axis)
    order = list(range(0, n, 2)) + list(range(1, n, 2))[::-1]
    ahead = [(order[i], order[(i + 1) % n]) for i in range(n)]
    across_ring = [(order[i], order[(i + n // 2) % n]) for i in range(n)]
    return ahead, [(b, a) for a, b in ahead], across_ring


def across(block, distance):
    n = lax.axis_size("blk")
    return lax.ppermute(block, "blk", [(i, i ^ distance) for i in range(n)])


def tied(block, *others):
    return lax.optimization_barrier((block, *others))[0]


def modulated(rows, factors):
    floats = rows.astype(F32)
    centre = floats - jnp.mean(floats, axis=-1, keepdims=True)
    spread = jnp.mean(centre * centre, axis=-1, keepdims=True)
    wide = factors.astype(F32)
    normed = centre / jnp.sqrt(spread + EPS_NORM)
    return normed * (1.0 + wide[1:2]) + wide[0:1]


def modulate_kernel(part_ref, *refs):
    sources, (left_ref, right_ref), landed = refs[:4], refs[4:6], refs[6:10]
    text_f32, sems = refs[10:]
    copies = [pltpu.make_async_copy(s, d, sems.at[i]) for i, (s, d) in enumerate(zip(sources, landed))]
    for copy in copies:
        copy.start()
    for copy in copies:
        copy.wait()
    video_ref, text_ref, vmod_ref, tmod_ref = landed
    text_rows = left_ref.shape[0] - video_ref.shape[0]
    half = left_ref.shape[1]
    text_f32[...] = text_ref[...].astype(F32)
    start = pl.multiple_of(part_ref[0] * text_rows, text_rows)
    own_text = text_f32[pl.ds(start, text_rows), :]
    video = modulated(video_ref[...], vmod_ref[...])
    text = modulated(own_text, tmod_ref[...])
    both = jnp.concatenate([video, text], axis=0).astype(BF16)
    left_ref[...] = both[:, :half]
    right_ref[...] = both[:, half:]


def fetch_kernel(count, *refs):
    many = (len(refs) - 1) // 2
    sources, landed, sems = refs[:many], refs[many : 2 * many], refs[-1]
    if count:
        step = sources[0].shape[1] // count
        sources = [s.at[:, i * step : (i + 1) * step, :] for s in sources for i in range(count)]
        landed = [s.at[:, i * step : (i + 1) * step, :] for s in landed for i in range(count)]
    copies = [pltpu.make_async_copy(s, d, sems.at[i]) for i, (s, d) in enumerate(zip(sources, landed))]
    for copy in copies:
        copy.start()
    for copy in copies:
        copy.wait()


def head_normed(mixture, gain):
    heads = []
    for h in range(mixture.shape[1] // HD):
        vectors = mixture[:, h * HD : (h + 1) * HD]
        inverse = lax.rsqrt(jnp.mean(vectors * vectors, axis=-1, keepdims=True) + EPS_NORM)
        heads.append(vectors * inverse * gain)
    return jnp.concatenate(heads, axis=1)


def project_kernel(shards, video_rows, *refs):
    chunks = refs[: 2 * shards]
    wv_ref, wt_ref, vgain_ref, tgain_ref, q_ref, kv_ref = refs[2 * shards :]
    width = q_ref.shape[1]
    video, text = [], []
    for side in range(2):
        floats = [chunks[2 * i + side][...].astype(F32) for i in range(shards)]
        video.append(jnp.concatenate([f[:video_rows] for f in floats], axis=0).astype(BF16))
        text.append(jnp.concatenate([f[video_rows:] for f in floats], axis=0).astype(BF16))
    half = video[0].shape[1]

    def mixed(sides, w_ref, j):
        total = jnp.dot(sides[0], w_ref[j, :half, :], preferred_element_type=F32)
        return total + jnp.dot(sides[1], w_ref[j, half:, :], preferred_element_type=F32)

    def joined(j, norm):
        v = mixed(video, wv_ref, j)
        t = mixed(text, wt_ref, j)
        if norm:
            v = head_normed(v, vgain_ref[j : j + 1, :])
            t = head_normed(t, tgain_ref[j : j + 1, :])
        return jnp.concatenate([v, t], axis=0).astype(BF16)

    q_ref[...] = joined(0, True)
    kv_ref[:, :width] = joined(1, True)
    kv_ref[:, width:] = joined(2, False)


def wide_rows(refs, counts):
    return jnp.concatenate([r[...].astype(F32)[:n] for r, n in zip(refs, counts)], axis=0).astype(BF16)


def absorbed(state, query, block):
    width = query.shape[1]
    factor = HD ** (-0.5) * math.log2(math.e)
    raised = []
    for h in range(width // HD):
        mine = slice(h * HD, (h + 1) * HD)
        scores = lax.dot_general(
            block[:, mine], query[:, mine], (((1,), (1,)), ((), ())), preferred_element_type=F32
        )
        highest = jnp.max(scores, axis=0, keepdims=True)
        if state:
            before, totals, sums = state[h]
            highest = jnp.maximum(before, highest)
        weights = jnp.exp2((scores - highest) * factor)
        total = jnp.sum(weights, axis=0, keepdims=True)
        mixed = lax.dot_general(
            block[:, width + h * HD : width + (h + 1) * HD],
            weights.astype(BF16),
            (((0,), (0,)), ((), ())),
            preferred_element_type=F32,
        )
        if state:
            shrink = jnp.exp2((before - highest) * factor)
            total = totals * shrink + total
            mixed = sums * shrink + mixed
        raised.append((highest, total, mixed))
    return raised


def load_state(stats_ref, sums_ref):
    heads = stats_ref.shape[0] // 2
    return [
        (
            stats_ref[h : h + 1, :],
            stats_ref[heads + h : heads + h + 1, :],
            sums_ref[h * HD : (h + 1) * HD, :],
        )
        for h in range(heads)
    ]


def attend_kernel(sizes, video_rows, with_text, fresh, queries, *refs):
    groups, sources = len(sizes), len(with_text)
    query = wide_rows(refs[:queries], [r.shape[0] for r in refs[:queries]])
    refs = refs[queries:]
    state = []
    if not fresh:
        state = load_state(*refs[:2])
        refs = refs[2:]
    pieces, outs = refs[: groups * sources], refs[groups * sources :]
    if fresh:
        outs[0][...] = query
    stats_ref, sums_ref = outs[-2:]
    for s in range(sources):
        held = pieces[s * groups : (s + 1) * groups]
        counts = [p.shape[0] if with_text[s] else n * video_rows for p, n in zip(held, sizes)]
        state = absorbed(state, query, wide_rows(held, counts))
    heads = len(state)
    for h, (highest, totals, sums) in enumerate(state):
        stats_ref[h : h + 1, :] = highest
        stats_ref[heads + h : heads + h + 1, :] = totals
        sums_ref[h * HD : (h + 1) * HD, :] = sums


def finish_kernel(sizes, video_rows, with_text, query_ref, stats_ref, sums_ref, *refs):
    sources = len(with_text)
    pieces, weights = refs[:sources], refs[sources : sources + 2]
    outs = refs[sources + 2 :]
    counts = [p.shape[0] if w else sizes[-1] * video_rows for p, w in zip(pieces, with_text)]
    state = absorbed(load_state(stats_ref, sums_ref), query_ref[...], wide_rows(pieces, counts))
    flat = jnp.concatenate([sums / totals for _, totals, sums in state], axis=0)
    rows_out = jnp.transpose(flat)
    text_rows = rows_out.shape[0] // sum(sizes) - video_rows
    video, text = [], []
    start = 0
    for size in sizes:
        video.append(rows_out[start : start + size * video_rows])
        start += size * video_rows
        text.append(rows_out[start : start + size * text_rows])
        start += size * text_rows
    video, text = [jnp.concatenate(rows, axis=0).astype(BF16) for rows in (video, text)]
    put_partials(outs, video, text, weights, sum(sizes))


def put_partials(outs, video, text, weights, shards):
    lead = outs[0].shape[1]
    cuts = [slice(0, lead), slice(lead, weights[0].shape[1])]
    vn, tn = video.shape[0] // shards, text.shape[0] // shards
    left, right = [jnp.dot(video, weights[0][:, c], preferred_element_type=F32) for c in cuts]
    bands = [
        jnp.dot(text, weights[1][:, c : c + lead], preferred_element_type=F32)
        for c in range(0, weights[1].shape[1], lead)
    ]
    for i in range(shards):
        rows = [left[i * vn : (i + 1) * vn]] + [y[i * tn : (i + 1) * tn] for y in bands]
        outs[2 * i][...] = jnp.concatenate(rows, axis=0).astype(BF16)
        outs[2 * i + 1][...] = right[i * vn : (i + 1) * vn].astype(BF16)


def close_text_kernel(fa_ref, ba_ref, own_ref, tmod_ref, text_ref):
    text_rows, width = text_ref.shape
    lead = own_ref.shape[1]
    start = own_ref.shape[0] - text_rows * (width // lead)
    total = sum(r[...].astype(F32)[start:] for r in (fa_ref, ba_ref, own_ref))
    for band in range(width // lead):
        columns = slice(band * lead, (band + 1) * lead)
        gate = tmod_ref[2:3, columns].astype(F32)
        text_ref[:, columns] = (total[band * text_rows : (band + 1) * text_rows] * gate).astype(BF16)


def close_kernel(part_ref, fa, ba, own_a, fb, bb, own_b, vmod_ref, *refs):
    pieces, (video_ref, text_ref, wide) = refs[:-3], refs[-3:]
    video_rows, width = video_ref.shape
    lead = own_a.shape[1]
    for columns, arrivals in ((slice(0, lead), (fa, ba, own_a)), (slice(lead, width), (fb, bb, own_b))):
        total = sum(r[...].astype(F32)[:video_rows] for r in arrivals)
        video_ref[:, columns] = (total * vmod_ref[2:3, columns].astype(F32)).astype(BF16)
    rows = pieces[0].shape[0]
    for d, piece in enumerate(pieces):
        start = pl.multiple_of((part_ref[0] ^ d) * rows, rows)
        wide[pl.ds(start, rows), :] = piece[...].astype(F32)
    text_ref[...] = wide[...].astype(BF16)


def local(
    video_tokens,
    text_tokens,
    video_modulation,
    text_modulation,
    video_projection,
    text_projection,
    video_output,
    text_output,
    video_gains,
    text_gains,
):
    n_blk, n_uly = lax.axis_size("blk"), lax.axis_size("uly")
    reach = n_uly // 2
    ahead, back, opposite = ring_routes("uly")
    video_rows, width = video_tokens.shape
    half = width // 2
    parts = math.gcd(n_blk, text_tokens.shape[0] // 8)
    text_rows = text_tokens.shape[0] // parts
    shard_rows = video_rows + text_rows
    cols = video_output.shape[0]
    part = lax.rem(lax.axis_index("blk"), parts).reshape(1).astype(jnp.int32)

    chunk = jax.ShapeDtypeStruct((shard_rows, half), BF16)
    own = call(
        modulate_kernel,
        [chunk, chunk],
        (part, video_tokens, text_tokens, video_modulation, text_modulation),
        8,
        [pltpu.VMEM(a.shape, BF16) for a in (video_tokens, text_tokens, video_modulation, text_modulation)]
        + [pltpu.VMEM(text_tokens.shape, F32), pltpu.SemaphoreType.DMA((4,))],
        smem=(0,),
        hbm=(1, 2, 3, 4),
    )

    def fetched(arrays, after, count=0):
        arrays = [tied(arrays[0], after), *arrays[1:]]
        return call(
            functools.partial(fetch_kernel, count),
            [jax.ShapeDtypeStruct(a.shape, a.dtype) for a in arrays],
            arrays,
            1,
            [pltpu.SemaphoreType.DMA((len(arrays) * max(count, 1),))],
            hbm=range(len(arrays)),
        )

    weights = [jnp.transpose(p, (1, 0, 2)) for p in (video_projection, text_projection)]
    held, ends, waiting = [], [], []
    queries, pieces, groups = [], [], []

    def fetch_all(after):
        held.extend(fetched(weights, after, 4))
        return held[-1]

    def fetch_rest(after):
        ends.extend(fetched([video_output, text_output, video_gains, text_gains], after))
        return ends[0]

    def project(after, direct=False):
        group = list(waiting)
        waiting.clear()
        rows = len(group) * shard_rows
        chunks = [c for _, *pair in group for c in pair]
        q, kv = call(
            functools.partial(project_kernel, len(group), video_rows),
            [
                jax.ShapeDtypeStruct((rows, cols), BF16),
                jax.ShapeDtypeStruct((rows, 2 * cols), BF16),
            ],
            [tied(chunks[0], after), *chunks[1:], *held, *ends[2:]],
            12,
            flops=2 * rows * width * 3 * cols,
        )
        if direct:
            spread = [kv] + [across(kv, d) for d in range(1, n_blk)]
        else:
            spread = {d: across(kv, d) if d else kv for d in (0, 1, *range(2, n_blk, 2))}
        queries.append(q)
        pieces.append(spread)
        groups.append(group)
        return q

    beside = {(1, 1): [fetch_all], (2, 0): [fetch_rest], (2, 1): [project], (3, 1): [project], (4, 1): [project]}
    fa, fb = own
    ba, bb = own
    waiting.append((0, *own))
    due = []
    for step in range(1, reach + 1):
        behind = fa
        fa = lax.ppermute(tied(fa, *due) if due else fa, "uly", ahead)
        bb = lax.ppermute(bb, "uly", back)
        due = [task(behind) for task in beside.get((step, 0), [])]
        if step < reach:
            behind = fb
            fb = lax.ppermute(tied(fb, *due) if due else fb, "uly", ahead)
            ba = lax.ppermute(ba, "uly", back)
            due = [task(behind) for task in beside.get((step, 1), [])]
            waiting += [(-step, fa, fb), (step, ba, bb)]
        else:
            due = [task(fb) for task in beside.get((step, 1), [])]
            waiting += [(reach, fa, bb)]
            project(fa, True)

    for spread in pieces[:-1]:
        for d in range(3, n_blk, 2):
            spread[d] = across(tied(spread[d - 1], queries[-1]), 1)

    sizes = [len(g) for g in groups]
    slots = [r for group in groups for r, *_ in group]
    total_rows = shard_rows * n_uly
    with_text = [d < parts for d in range(n_blk)]
    state = [
        jax.ShapeDtypeStruct((2 * cols // HD, total_rows), F32),
        jax.ShapeDtypeStruct((cols, total_rows), F32),
    ]
    query, *carried = call(
        functools.partial(attend_kernel, sizes[:-1], video_rows, with_text[:2], True, len(queries)),
        [jax.ShapeDtypeStruct((total_rows, cols), BF16), *state],
        queries + [spread[d] for d in range(2) for spread in pieces[:-1]],
        16,
        flops=8 * total_rows * (total_rows - shard_rows) * cols,
    )
    carried = call(
        functools.partial(attend_kernel, sizes[:-1], video_rows, with_text[2:], False, 1),
        state,
        [query, *carried] + [spread[d] for d in range(2, n_blk) for spread in pieces[:-1]],
        16,
        flops=4 * total_rows * (total_rows - shard_rows) * (n_blk - 2) * cols,
    )
    lead = width // 3
    left_rows = video_rows + text_rows * (width // lead)
    shapes = [
        jax.ShapeDtypeStruct((left_rows, lead), BF16),
        jax.ShapeDtypeStruct((video_rows, width - lead), BF16),
    ]
    partial = call(
        functools.partial(finish_kernel, sizes, video_rows, with_text),
        shapes * n_uly,
        [query, *carried] + pieces[-1] + ends[:2],
        16,
        flops=2 * total_rows * cols * width,
    )
    mine = {r: (partial[2 * i], partial[2 * i + 1]) for i, r in enumerate(slots)}
    mine[-reach] = mine[reach]

    def joined(arriving, own_part):
        return (arriving.astype(F32) + own_part.astype(F32)).astype(BF16)

    fa, bb = mine[reach][0], mine[-reach][1]
    fb, ba = mine[reach - 1][1], mine[1 - reach][0]
    for left in range(reach - 1, -1, -1):
        fa = lax.ppermute(fa, "uly", ahead)
        bb = lax.ppermute(bb, "uly", back)
        if left:
            fa = joined(fa, mine[left][0])
            bb = joined(bb, mine[-left][1])
            fb = lax.ppermute(fb, "uly", ahead)
            ba = lax.ppermute(ba, "uly", back)
            if left > 1:
                fb = joined(fb, mine[left - 1][1])
                ba = joined(ba, mine[1 - left][0])
    text_part = call(
        close_text_kernel,
        jax.ShapeDtypeStruct((text_rows, width), BF16),
        (fa, ba, mine[0][0], text_modulation),
        4,
    )
    pieces = [text_part] + [across(text_part, d) for d in range(1, parts)]
    return tuple(
        call(
            close_kernel,
            [jax.ShapeDtypeStruct(t.shape, BF16) for t in (video_tokens, text_tokens)],
            (part, fa, ba, mine[0][0], fb, bb, mine[0][1], video_modulation, *pieces),
            8,
            [pltpu.VMEM(text_tokens.shape, F32)],
            smem=(0,),
        )
    )


def solution(mesh):
    placed = (
        P(("blk", "uly"), None),
        P("uly", None),
        P(),
        P(),
        P(None, None, "uly"),
        P(None, None, "uly"),
        P("uly", None),
        P("uly", None),
        P(),
        P(),
    )
    return jax.shard_map(
        local,
        mesh=mesh,
        in_specs=placed,
        out_specs=(P(("blk", "uly"), None), P("uly", None)),
        check_vma=False,
    )
```

```python
import functools
import math

import jax
import jax.numpy as jnp
from jax import lax
from jax.experimental import pallas as pl
from jax.experimental.pallas import tpu as pltpu
from jax.sharding import PartitionSpec as P

HD = 128
EPS_NORM = 1e-06
F32 = jnp.float32
BF16 = jnp.bfloat16
VMEM = pl.BlockSpec(memory_space=pltpu.VMEM)
HBM = pl.BlockSpec(memory_space=pltpu.HBM)
SMEM = pl.BlockSpec(memory_space=pltpu.SMEM)


def call(kernel, outs, args, vmem_mib, scratch=(), flops=0, smem=(), hbm=()):
    moved = sum(a.size * a.dtype.itemsize for a in args)
    args = [pltpu.with_memory_space_constraint(a, pltpu.HBM) if i in hbm else a for i, a in enumerate(args)]
    return pl.pallas_call(
        kernel,
        out_shape=outs,
        in_specs=[SMEM if i in smem else HBM if i in hbm else VMEM for i in range(len(args))],
        out_specs=jax.tree.map(lambda _: VMEM, outs),
        scratch_shapes=list(scratch),
        compiler_params=pltpu.CompilerParams(vmem_limit_bytes=vmem_mib << 20),
        cost_estimate=pl.CostEstimate(flops=flops, bytes_accessed=moved, transcendentals=0),
    )(*args)


def ring_routes(axis):
    n = lax.axis_size(axis)
    order = list(range(0, n, 2)) + list(range(1, n, 2))[::-1]
    ahead = [(order[i], order[(i + 1) % n]) for i in range(n)]
    return ahead, [(b, a) for a, b in ahead]


def across(block, distance):
    n = lax.axis_size("blk")
    return lax.ppermute(block, "blk", [(i, i ^ distance) for i in range(n)])


def tied(block, *others):
    return lax.optimization_barrier((block, *others))[0]


def modulated(rows, factors):
    floats = rows.astype(F32)
    centre = floats - jnp.mean(floats, axis=-1, keepdims=True)
    spread = jnp.mean(centre * centre, axis=-1, keepdims=True)
    wide = factors.astype(F32)
    normed = centre / jnp.sqrt(spread + EPS_NORM)
    return normed * (1.0 + wide[1:2]) + wide[0:1]


def modulate_kernel(part_ref, *refs):
    sources, (left_ref, right_ref), landed = refs[:4], refs[4:6], refs[6:10]
    text_f32, sems = refs[10:]
    copies = [pltpu.make_async_copy(s, d, sems.at[i]) for i, (s, d) in enumerate(zip(sources, landed))]
    for copy in copies:
        copy.start()
    for copy in copies:
        copy.wait()
    video_ref, text_ref, vmod_ref, tmod_ref = landed
    text_rows = left_ref.shape[0] - video_ref.shape[0]
    half = left_ref.shape[1]
    text_f32[...] = text_ref[...].astype(F32)
    start = pl.multiple_of(part_ref[0] * text_rows, text_rows)
    own_text = text_f32[pl.ds(start, text_rows), :]
    video = modulated(video_ref[...], vmod_ref[...])
    text = modulated(own_text, tmod_ref[...])
    both = jnp.concatenate([video, text], axis=0).astype(BF16)
    left_ref[...] = both[:, :half]
    right_ref[...] = both[:, half:]


def bands(array, count):
    step = array.shape[-2] // count
    return [array.at[..., i * step : (i + 1) * step, :] for i in range(count)]


def fetch_kernel(counts, *refs):
    many = len(counts)
    copies = []
    for source, landed, count in zip(refs[:many], refs[many : 2 * many], counts):
        for pair in zip(bands(source, count), bands(landed, count)):
            copies.append(pltpu.make_async_copy(*pair, refs[-1].at[len(copies)]))
    for copy in copies:
        copy.start()
    for copy in copies:
        copy.wait()


def head_normed(mixture, gain):
    heads = []
    for h in range(mixture.shape[1] // HD):
        vectors = mixture[:, h * HD : (h + 1) * HD]
        inverse = lax.rsqrt(jnp.mean(vectors * vectors, axis=-1, keepdims=True) + EPS_NORM)
        heads.append(vectors * inverse * gain)
    return jnp.concatenate(heads, axis=1)


def project_kernel(shards, video_rows, *refs):
    chunks = refs[: 2 * shards]
    wv_ref, wt_ref, vgain_ref, tgain_ref, q_ref, kv_ref = refs[2 * shards :]
    width = q_ref.shape[1]
    video, text = [], []
    for side in range(2):
        floats = [chunks[2 * i + side][...].astype(F32) for i in range(shards)]
        video.append(jnp.concatenate([f[:video_rows] for f in floats], axis=0).astype(BF16))
        text.append(jnp.concatenate([f[video_rows:] for f in floats], axis=0).astype(BF16))
    half = video[0].shape[1]

    def mixed(sides, w_ref, j):
        total = jnp.dot(sides[0], w_ref[j, :half, :], preferred_element_type=F32)
        return total + jnp.dot(sides[1], w_ref[j, half:, :], preferred_element_type=F32)

    def joined(j, norm):
        v = mixed(video, wv_ref, j)
        t = mixed(text, wt_ref, j)
        if norm:
            v = head_normed(v, vgain_ref[j : j + 1, :])
            t = head_normed(t, tgain_ref[j : j + 1, :])
        return jnp.concatenate([v, t], axis=0).astype(BF16)

    q_ref[...] = joined(0, True)
    kv_ref[:, :width] = joined(1, True)
    kv_ref[:, width:] = joined(2, False)


def wide_rows(refs, counts):
    return jnp.concatenate([r[...].astype(F32)[:n] for r, n in zip(refs, counts)], axis=0).astype(BF16)


def absorbed(state, query, block):
    width = query.shape[1]
    factor = HD ** (-0.5) * math.log2(math.e)
    raised = []
    for h in range(width // HD):
        mine = slice(h * HD, (h + 1) * HD)
        scores = lax.dot_general(
            block[:, mine], query[:, mine], (((1,), (1,)), ((), ())), preferred_element_type=F32
        )
        highest = jnp.max(scores, axis=0, keepdims=True)
        if state:
            before, totals, sums = state[h]
            highest = jnp.maximum(before, highest)
        weights = jnp.exp2((scores - highest) * factor)
        total = jnp.sum(weights, axis=0, keepdims=True)
        mixed = lax.dot_general(
            block[:, width + h * HD : width + (h + 1) * HD],
            weights.astype(BF16),
            (((0,), (0,)), ((), ())),
            preferred_element_type=F32,
        )
        if state:
            shrink = jnp.exp2((before - highest) * factor)
            total = totals * shrink + total
            mixed = sums * shrink + mixed
        raised.append((highest, total, mixed))
    return raised


def load_state(stats_ref, sums_ref):
    heads = stats_ref.shape[0] // 2
    return [
        (
            stats_ref[h : h + 1, :],
            stats_ref[heads + h : heads + h + 1, :],
            sums_ref[h * HD : (h + 1) * HD, :],
        )
        for h in range(heads)
    ]


def absorb_blocks(state, query, blocks, pieces):
    start = 0
    for counts in blocks:
        held = pieces[start : start + len(counts)]
        state = absorbed(state, query, wide_rows(held, counts))
        start += len(counts)
    return state


def attend_kernel(blocks, queries, *refs):
    if queries:
        query = wide_rows(refs[:queries], [r.shape[0] for r in refs[:queries]])
        pieces, (query_ref, stats_ref, sums_ref) = refs[queries:-3], refs[-3:]
        query_ref[...] = query
        state = absorb_blocks([], query, blocks, pieces)
    else:
        query, state = refs[0][...], load_state(*refs[1:3])
        pieces, (stats_ref, sums_ref) = refs[3:-2], refs[-2:]
        state = absorb_blocks(state, query, blocks, pieces)
    heads = len(state)
    for h, (highest, totals, sums) in enumerate(state):
        stats_ref[h : h + 1, :] = highest
        stats_ref[heads + h : heads + h + 1, :] = totals
        sums_ref[h * HD : (h + 1) * HD, :] = sums


def finish_kernel(blocks, sizes, video_rows, query_ref, stats_ref, sums_ref, *refs):
    held = sum(len(counts) for counts in blocks)
    pieces, weights, outs = refs[:held], refs[held : held + 2], refs[held + 2 :]
    state = absorb_blocks(load_state(stats_ref, sums_ref), query_ref[...], blocks, pieces)
    flat = jnp.concatenate([sums / totals for _, totals, sums in state], axis=0)
    rows_out = jnp.transpose(flat)
    text_rows = rows_out.shape[0] // sum(sizes) - video_rows
    video, text = [], []
    start = 0
    for size in sizes:
        video.append(rows_out[start : start + size * video_rows])
        start += size * video_rows
        text.append(rows_out[start : start + size * text_rows])
        start += size * text_rows
    video, text = [jnp.concatenate(rows, axis=0).astype(BF16) for rows in (video, text)]
    put_partials(outs, video, text, weights, sum(sizes))


def put_partials(outs, video, text, weights, shards):
    lead = outs[0].shape[1]
    cuts = [slice(0, lead), slice(lead, weights[0].shape[1])]
    vn, tn = video.shape[0] // shards, text.shape[0] // shards
    left, right = [jnp.dot(video, weights[0][:, c], preferred_element_type=F32) for c in cuts]
    bands = [
        jnp.dot(text, weights[1][:, c : c + lead], preferred_element_type=F32)
        for c in range(0, weights[1].shape[1], lead)
    ]
    for i in range(shards):
        rows = [left[i * vn : (i + 1) * vn]] + [y[i * tn : (i + 1) * tn] for y in bands]
        outs[2 * i][...] = jnp.concatenate(rows, axis=0).astype(BF16)
        outs[2 * i + 1][...] = right[i * vn : (i + 1) * vn].astype(BF16)


def close_text_kernel(fa_ref, ba_ref, own_ref, tmod_ref, text_ref):
    text_rows, width = text_ref.shape
    lead = own_ref.shape[1]
    start = own_ref.shape[0] - text_rows * (width // lead)
    total = sum(r[...].astype(F32)[start:] for r in (fa_ref, ba_ref, own_ref))
    for band in range(width // lead):
        columns = slice(band * lead, (band + 1) * lead)
        gate = tmod_ref[2:3, columns].astype(F32)
        text_ref[:, columns] = (total[band * text_rows : (band + 1) * text_rows] * gate).astype(BF16)


def close_kernel(part_ref, fa, ba, own_a, fb, bb, own_b, vmod_ref, *refs):
    pieces, (video_ref, text_ref, wide) = refs[:-3], refs[-3:]
    video_rows, width = video_ref.shape
    lead = own_a.shape[1]
    for columns, arrivals in ((slice(0, lead), (fa, ba, own_a)), (slice(lead, width), (fb, bb, own_b))):
        total = sum(r[...].astype(F32)[:video_rows] for r in arrivals)
        video_ref[:, columns] = (total * vmod_ref[2:3, columns].astype(F32)).astype(BF16)
    rows = pieces[0].shape[0]
    for d, piece in enumerate(pieces):
        start = pl.multiple_of((part_ref[0] ^ d) * rows, rows)
        wide[pl.ds(start, rows), :] = piece[...].astype(F32)
    text_ref[...] = wide[...].astype(BF16)


def local(
    video_tokens,
    text_tokens,
    video_modulation,
    text_modulation,
    video_projection,
    text_projection,
    video_output,
    text_output,
    video_gains,
    text_gains,
):
    n_blk, n_uly = lax.axis_size("blk"), lax.axis_size("uly")
    reach = n_uly // 2
    ahead, back = ring_routes("uly")
    video_rows, width = video_tokens.shape
    half = width // 2
    parts = math.gcd(n_blk, text_tokens.shape[0] // 8)
    text_rows = text_tokens.shape[0] // parts
    shard_rows = video_rows + text_rows
    cols = video_output.shape[0]
    part = lax.rem(lax.axis_index("blk"), parts).reshape(1).astype(jnp.int32)

    chunk = jax.ShapeDtypeStruct((shard_rows, half), BF16)
    own = call(
        modulate_kernel,
        [chunk, chunk],
        (part, video_tokens, text_tokens, video_modulation, text_modulation),
        8,
        [pltpu.VMEM(a.shape, BF16) for a in (video_tokens, text_tokens, video_modulation, text_modulation)]
        + [pltpu.VMEM(text_tokens.shape, F32), pltpu.SemaphoreType.DMA((4,))],
        smem=(0,),
        hbm=(1, 2, 3, 4),
    )

    def fetched(arrays, counts, after):
        arrays = [tied(arrays[0], after), *arrays[1:]]
        return call(
            functools.partial(fetch_kernel, counts),
            [jax.ShapeDtypeStruct(a.shape, a.dtype) for a in arrays],
            arrays,
            1,
            [pltpu.SemaphoreType.DMA((sum(counts),))],
            hbm=range(len(arrays)),
        )

    weights, gains, ends = [], [], []
    waiting = []
    queries, pieces, groups = [], [], []

    def fetch_first(after):
        held = [jnp.transpose(p, (1, 0, 2)) for p in (video_projection, text_projection)]
        *held, vgains, tgains = fetched([*held, video_gains, text_gains], [4, 4, 1, 1], after)
        weights.extend(held)
        gains.extend((vgains, tgains))
        return held[0]

    def fetch_last(after):
        ends.extend(fetched([video_output, text_output], [2, 2], after))
        return ends[0]

    def project(after, direct=False):
        group = list(waiting)
        waiting.clear()
        rows = len(group) * shard_rows
        chunks = [c for _, *pair in group for c in pair]
        q, kv = call(
            functools.partial(project_kernel, len(group), video_rows),
            [
                jax.ShapeDtypeStruct((rows, cols), BF16),
                jax.ShapeDtypeStruct((rows, 2 * cols), BF16),
            ],
            [tied(chunks[0], after), *chunks[1:], *weights, *gains],
            12,
            flops=2 * rows * width * 3 * cols,
        )
        if direct:
            spread = [kv] + [across(kv, d) for d in range(1, n_blk)]
        else:
            spread = {d: across(kv, d) if d else kv for d in (0, 1, *range(2, n_blk, 2))}
        queries.append(q)
        pieces.append(spread)
        groups.append(group)
        return q

    beside = {(1, 1): [fetch_first], (2, 1): [project], (3, 1): [project], (4, 1): [project]}
    fa, fb = own
    ba, bb = own
    waiting.append((0, *own))
    due = []
    for step in range(1, reach + 1):
        behind = fa
        fa = lax.ppermute(tied(fa, *due) if due else fa, "uly", ahead)
        bb = lax.ppermute(bb, "uly", back)
        due = [task(behind) for task in beside.get((step, 0), [])]
        if step < reach:
            behind = fb
            fb = lax.ppermute(tied(fb, *due) if due else fb, "uly", ahead)
            ba = lax.ppermute(ba, "uly", back)
            due = [task(behind) for task in beside.get((step, 1), [])]
            waiting += [(-step, fa, fb), (step, ba, bb)]
        else:
            due = [task(fb) for task in beside.get((step, 1), [])]
            waiting += [(reach, fa, bb)]
            project(fa, True)

    def second_leg(spread, after):
        for d in range(3, n_blk, 2):
            if isinstance(spread, dict):
                spread[d] = across(tied(spread[d - 1], after), 1)

    for spread in pieces[:-1]:
        second_leg(spread, queries[-1])
    sizes = [len(g) for g in groups]
    slots = [r for group in groups for r, *_ in group]
    total_rows = shard_rows * n_uly

    def some(sources, chosen):
        return [
            [(pieces[g][d], sizes[g] * (shard_rows if d < parts else video_rows)) for g in chosen]
            for d in sources
        ]

    def attended(blocks, given, queries, kernel, outs, extra=(), more=0):
        counts = [[n for _, n in block] for block in blocks]
        keys = [piece for block in blocks for piece, _ in block]
        return call(
            functools.partial(kernel, counts, *queries),
            outs,
            [*given, *keys, *extra],
            16,
            flops=4 * total_rows * sum(map(sum, counts)) * cols + more,
        )

    state = [
        jax.ShapeDtypeStruct((2 * cols // HD, total_rows), F32),
        jax.ShapeDtypeStruct((cols, total_rows), F32),
    ]
    first = range(len(groups) - 1)
    outer = range(2, n_blk)
    query, *carried = attended(
        some((0, 1), first),
        queries,
        (len(queries),),
        attend_kernel,
        [jax.ShapeDtypeStruct((total_rows, cols), BF16), *state],
    )
    carried = attended(some(outer, first[:-1]), [query, *carried], (0,), attend_kernel, state)
    lead = width // 3
    left_rows = video_rows + text_rows * (width // lead)
    shapes = [
        jax.ShapeDtypeStruct((left_rows, lead), BF16),
        jax.ShapeDtypeStruct((video_rows, width - lead), BF16),
    ]
    last = [piece for block in some(outer, first[-1:]) + some(range(n_blk), (len(groups) - 1,)) for piece in block]
    partial = attended(
        [last],
        [query, *carried],
        (sizes, video_rows),
        finish_kernel,
        shapes * n_uly,
        (video_output, text_output),
        2 * total_rows * cols * width,
    )
    mine = {r: (partial[2 * i], partial[2 * i + 1]) for i, r in enumerate(slots)}
    mine[-reach] = mine[reach]

    def joined(arriving, own_part):
        return (arriving.astype(F32) + own_part.astype(F32)).astype(BF16)

    fa, bb = mine[reach][0], mine[-reach][1]
    fb, ba = mine[reach - 1][1], mine[1 - reach][0]
    for left in range(reach - 1, -1, -1):
        fa = lax.ppermute(fa, "uly", ahead)
        bb = lax.ppermute(bb, "uly", back)
        if left:
            fa = joined(fa, mine[left][0])
            bb = joined(bb, mine[-left][1])
            fb = lax.ppermute(fb, "uly", ahead)
            ba = lax.ppermute(ba, "uly", back)
            if left > 1:
                fb = joined(fb, mine[left - 1][1])
                ba = joined(ba, mine[1 - left][0])
    text_part = call(
        close_text_kernel,
        jax.ShapeDtypeStruct((text_rows, width), BF16),
        (fa, ba, mine[0][0], text_modulation),
        4,
    )
    pieces = [text_part] + [across(text_part, d) for d in range(1, parts)]
    return tuple(
        call(
            close_kernel,
            [jax.ShapeDtypeStruct(t.shape, BF16) for t in (video_tokens, text_tokens)],
            (part, fa, ba, mine[0][0], fb, bb, mine[0][1], video_modulation, *pieces),
            8,
            [pltpu.VMEM(text_tokens.shape, F32)],
            smem=(0,),
        )
    )


def solution(mesh):
    placed = (
        P(("blk", "uly"), None),
        P("uly", None),
        P(),
        P(),
        P(None, None, "uly"),
        P(None, None, "uly"),
        P("uly", None),
        P("uly", None),
        P(),
        P(),
    )
    return jax.shard_map(
        local,
        mesh=mesh,
        in_specs=placed,
        out_specs=(P(("blk", "uly"), None), P("uly", None)),
        check_vma=False,
    )
```

```python
import functools
import math

import jax
import jax.numpy as jnp
from jax import lax
from jax.experimental import pallas as pl
from jax.experimental.pallas import tpu as pltpu
from jax.sharding import PartitionSpec as P

HD = 128
EPS_NORM = 1e-06
F32 = jnp.float32
BF16 = jnp.bfloat16
VMEM = pl.BlockSpec(memory_space=pltpu.VMEM)
HBM = pl.BlockSpec(memory_space=pltpu.HBM)
SMEM = pl.BlockSpec(memory_space=pltpu.SMEM)


def call(kernel, outs, args, vmem_mib, scratch=(), flops=0, smem=(), hbm=()):
    moved = sum(a.size * a.dtype.itemsize for a in args)
    args = [pltpu.with_memory_space_constraint(a, pltpu.HBM) if i in hbm else a for i, a in enumerate(args)]
    return pl.pallas_call(
        kernel,
        out_shape=outs,
        in_specs=[SMEM if i in smem else HBM if i in hbm else VMEM for i in range(len(args))],
        out_specs=jax.tree.map(lambda _: VMEM, outs),
        scratch_shapes=list(scratch),
        compiler_params=pltpu.CompilerParams(vmem_limit_bytes=vmem_mib << 20),
        cost_estimate=pl.CostEstimate(flops=flops, bytes_accessed=moved, transcendentals=0),
    )(*args)


def ring_routes(axis):
    n = lax.axis_size(axis)
    order = list(range(0, n, 2)) + list(range(1, n, 2))[::-1]
    ahead = [(order[i], order[(i + 1) % n]) for i in range(n)]
    return ahead, [(b, a) for a, b in ahead]


def across(block, distance):
    n = lax.axis_size("blk")
    return lax.ppermute(block, "blk", [(i, i ^ distance) for i in range(n)])


def tied(block, *others):
    return lax.optimization_barrier((block, *others))[0]


def modulated(rows, factors):
    floats = rows.astype(F32)
    centre = floats - jnp.mean(floats, axis=-1, keepdims=True)
    spread = jnp.mean(centre * centre, axis=-1, keepdims=True)
    wide = factors.astype(F32)
    normed = centre / jnp.sqrt(spread + EPS_NORM)
    return normed * (1.0 + wide[1:2]) + wide[0:1]


def modulate_kernel(part_ref, *refs):
    sources, (left_ref, right_ref), landed = refs[:4], refs[4:6], refs[6:10]
    text_f32, sems = refs[10:]
    copies = [pltpu.make_async_copy(s, d, sems.at[i]) for i, (s, d) in enumerate(zip(sources, landed))]
    for copy in copies:
        copy.start()
    for copy in copies:
        copy.wait()
    video_ref, text_ref, vmod_ref, tmod_ref = landed
    text_rows = left_ref.shape[0] - video_ref.shape[0]
    half = left_ref.shape[1]
    text_f32[...] = text_ref[...].astype(F32)
    start = pl.multiple_of(part_ref[0] * text_rows, text_rows)
    own_text = text_f32[pl.ds(start, text_rows), :]
    video = modulated(video_ref[...], vmod_ref[...])
    text = modulated(own_text, tmod_ref[...])
    both = jnp.concatenate([video, text], axis=0).astype(BF16)
    left_ref[...] = both[:, :half]
    right_ref[...] = both[:, half:]


def bands(array, count):
    step = array.shape[-2] // count
    return [array.at[..., i * step : (i + 1) * step, :] for i in range(count)]


def fetch_kernel(counts, *refs):
    many = len(counts)
    copies = []
    for source, landed, count in zip(refs[:many], refs[many : 2 * many], counts):
        for pair in zip(bands(source, count), bands(landed, count)):
            copies.append(pltpu.make_async_copy(*pair, refs[-1].at[len(copies)]))
    for copy in copies:
        copy.start()
    for copy in copies:
        copy.wait()


def head_normed(mixture, gain):
    heads = []
    for h in range(mixture.shape[1] // HD):
        vectors = mixture[:, h * HD : (h + 1) * HD]
        inverse = lax.rsqrt(jnp.mean(vectors * vectors, axis=-1, keepdims=True) + EPS_NORM)
        heads.append(vectors * inverse * gain)
    return jnp.concatenate(heads, axis=1)


def project_kernel(shards, video_rows, *refs):
    chunks = refs[: 2 * shards]
    wv_ref, wt_ref, vgain_ref, tgain_ref, q_ref, kv_ref = refs[2 * shards :]
    width = q_ref.shape[1]
    video, text = [], []
    for side in range(2):
        floats = [chunks[2 * i + side][...].astype(F32) for i in range(shards)]
        video.append(jnp.concatenate([f[:video_rows] for f in floats], axis=0).astype(BF16))
        text.append(jnp.concatenate([f[video_rows:] for f in floats], axis=0).astype(BF16))
    half = video[0].shape[1]

    def mixed(sides, w_ref, j):
        total = jnp.dot(sides[0], w_ref[j, :half, :], preferred_element_type=F32)
        return total + jnp.dot(sides[1], w_ref[j, half:, :], preferred_element_type=F32)

    def joined(j, norm):
        v = mixed(video, wv_ref, j)
        t = mixed(text, wt_ref, j)
        if norm:
            v = head_normed(v, vgain_ref[j : j + 1, :])
            t = head_normed(t, tgain_ref[j : j + 1, :])
        return jnp.concatenate([v, t], axis=0).astype(BF16)

    q_ref[...] = joined(0, True)
    kv_ref[:, :width] = joined(1, True)
    kv_ref[:, width:] = joined(2, False)


def wide_rows(refs, counts):
    return jnp.concatenate([r[...].astype(F32)[:n] for r, n in zip(refs, counts)], axis=0).astype(BF16)


def absorbed(state, query, block):
    width = query.shape[1]
    factor = HD ** (-0.5) * math.log2(math.e)
    raised = []
    for h in range(width // HD):
        mine = slice(h * HD, (h + 1) * HD)
        scores = lax.dot_general(
            block[:, mine], query[:, mine], (((1,), (1,)), ((), ())), preferred_element_type=F32
        )
        highest = jnp.max(scores, axis=0, keepdims=True)
        if state:
            before, totals, sums = state[h]
            highest = jnp.maximum(before, highest)
        weights = jnp.exp2((scores - highest) * factor)
        total = jnp.sum(weights, axis=0, keepdims=True)
        mixed = lax.dot_general(
            block[:, width + h * HD : width + (h + 1) * HD],
            weights.astype(BF16),
            (((0,), (0,)), ((), ())),
            preferred_element_type=F32,
        )
        if state:
            shrink = jnp.exp2((before - highest) * factor)
            total = totals * shrink + total
            mixed = sums * shrink + mixed
        raised.append((highest, total, mixed))
    return raised


def load_state(stats_ref, sums_ref):
    heads = stats_ref.shape[0] // 2
    return [
        (
            stats_ref[h : h + 1, :],
            stats_ref[heads + h : heads + h + 1, :],
            sums_ref[h * HD : (h + 1) * HD, :],
        )
        for h in range(heads)
    ]


def absorb_blocks(state, query, blocks, pieces):
    start = 0
    for counts in blocks:
        held = pieces[start : start + len(counts)]
        state = absorbed(state, query, wide_rows(held, counts))
        start += len(counts)
    return state


def attend_kernel(blocks, queries, *refs):
    if queries:
        query = wide_rows(refs[:queries], [r.shape[0] for r in refs[:queries]])
        pieces, (query_ref, stats_ref, sums_ref) = refs[queries:-3], refs[-3:]
        query_ref[...] = query
        state = absorb_blocks([], query, blocks, pieces)
    else:
        query, state = refs[0][...], load_state(*refs[1:3])
        pieces, (stats_ref, sums_ref) = refs[3:-2], refs[-2:]
        state = absorb_blocks(state, query, blocks, pieces)
    heads = len(state)
    for h, (highest, totals, sums) in enumerate(state):
        stats_ref[h : h + 1, :] = highest
        stats_ref[heads + h : heads + h + 1, :] = totals
        sums_ref[h * HD : (h + 1) * HD, :] = sums


def finish_kernel(blocks, sizes, video_rows, query_ref, stats_ref, sums_ref, *refs):
    held = sum(len(counts) for counts in blocks)
    pieces, weights, outs = refs[:held], refs[held : held + 2], refs[held + 2 :]
    state = absorb_blocks(load_state(stats_ref, sums_ref), query_ref[...], blocks, pieces)
    flat = jnp.concatenate([sums / totals for _, totals, sums in state], axis=0)
    rows_out = jnp.transpose(flat)
    text_rows = rows_out.shape[0] // sum(sizes) - video_rows
    video, text = [], []
    start = 0
    for size in sizes:
        video.append(rows_out[start : start + size * video_rows])
        start += size * video_rows
        text.append(rows_out[start : start + size * text_rows])
        start += size * text_rows
    video, text = [jnp.concatenate(rows, axis=0).astype(BF16) for rows in (video, text)]
    video_ref, *outs = outs
    video_ref[...] = video
    lead = outs[0].shape[1]
    left = jnp.dot(video, weights[0][:, :lead], preferred_element_type=F32)
    bands = [
        jnp.dot(text, weights[1][:, c : c + lead], preferred_element_type=F32)
        for c in range(0, weights[1].shape[1], lead)
    ]
    for i, out in enumerate(outs):
        rows = [left[i * video_rows : (i + 1) * video_rows]]
        rows += [y[i * text_rows : (i + 1) * text_rows] for y in bands]
        out[...] = jnp.concatenate(rows, axis=0).astype(BF16)


def right_kernel(video_ref, wv_ref, *outs):
    video_rows, columns = outs[0].shape
    lead = wv_ref.shape[1] - columns
    right = jnp.dot(video_ref[...], wv_ref[:, lead:], preferred_element_type=F32)
    for i, out in enumerate(outs):
        out[...] = right[i * video_rows : (i + 1) * video_rows].astype(BF16)


def close_text_kernel(fa_ref, ba_ref, own_ref, tmod_ref, text_ref):
    text_rows, width = text_ref.shape
    lead = own_ref.shape[1]
    start = own_ref.shape[0] - text_rows * (width // lead)
    total = sum(r[...].astype(F32)[start:] for r in (fa_ref, ba_ref, own_ref))
    for band in range(width // lead):
        columns = slice(band * lead, (band + 1) * lead)
        gate = tmod_ref[2:3, columns].astype(F32)
        text_ref[:, columns] = (total[band * text_rows : (band + 1) * text_rows] * gate).astype(BF16)


def close_kernel(part_ref, fa, ba, own_a, fb, bb, own_b, vmod_ref, *refs):
    pieces, (video_ref, text_ref, wide) = refs[:-3], refs[-3:]
    video_rows, width = video_ref.shape
    lead = own_a.shape[1]
    for columns, arrivals in ((slice(0, lead), (fa, ba, own_a)), (slice(lead, width), (fb, bb, own_b))):
        total = sum(r[...].astype(F32)[:video_rows] for r in arrivals)
        video_ref[:, columns] = (total * vmod_ref[2:3, columns].astype(F32)).astype(BF16)
    rows = pieces[0].shape[0]
    for d, piece in enumerate(pieces):
        start = pl.multiple_of((part_ref[0] ^ d) * rows, rows)
        wide[pl.ds(start, rows), :] = piece[...].astype(F32)
    text_ref[...] = wide[...].astype(BF16)


def local(
    video_tokens,
    text_tokens,
    video_modulation,
    text_modulation,
    video_projection,
    text_projection,
    video_output,
    text_output,
    video_gains,
    text_gains,
):
    n_blk, n_uly = lax.axis_size("blk"), lax.axis_size("uly")
    reach = n_uly // 2
    ahead, back = ring_routes("uly")
    video_rows, width = video_tokens.shape
    half = width // 2
    parts = math.gcd(n_blk, text_tokens.shape[0] // 8)
    text_rows = text_tokens.shape[0] // parts
    shard_rows = video_rows + text_rows
    cols = video_output.shape[0]
    part = lax.rem(lax.axis_index("blk"), parts).reshape(1).astype(jnp.int32)

    chunk = jax.ShapeDtypeStruct((shard_rows, half), BF16)
    own = call(
        modulate_kernel,
        [chunk, chunk],
        (part, video_tokens, text_tokens, video_modulation, text_modulation),
        8,
        [pltpu.VMEM(a.shape, BF16) for a in (video_tokens, text_tokens, video_modulation, text_modulation)]
        + [pltpu.VMEM(text_tokens.shape, F32), pltpu.SemaphoreType.DMA((4,))],
        smem=(0,),
        hbm=(1, 2, 3, 4),
    )

    def fetched(arrays, counts, after):
        arrays = [tied(arrays[0], after), *arrays[1:]]
        return call(
            functools.partial(fetch_kernel, counts),
            [jax.ShapeDtypeStruct(a.shape, a.dtype) for a in arrays],
            arrays,
            1,
            [pltpu.SemaphoreType.DMA((sum(counts),))],
            hbm=range(len(arrays)),
        )

    weights, gains, ends = [], [], []
    waiting = []
    queries, pieces, groups = [], [], []

    def fetch_first(after):
        held = [jnp.transpose(p, (1, 0, 2)) for p in (video_projection, text_projection)]
        *held, vgains, tgains = fetched([*held, video_gains, text_gains], [4, 4, 1, 1], after)
        weights.extend(held)
        gains.extend((vgains, tgains))
        return held[0]

    def fetch_last(after):
        ends.extend(fetched([video_output, text_output], [2, 2], after))
        return ends[0]

    def project(after, direct=False):
        group = list(waiting)
        waiting.clear()
        rows = len(group) * shard_rows
        chunks = [c for _, *pair in group for c in pair]
        q, kv = call(
            functools.partial(project_kernel, len(group), video_rows),
            [
                jax.ShapeDtypeStruct((rows, cols), BF16),
                jax.ShapeDtypeStruct((rows, 2 * cols), BF16),
            ],
            [tied(chunks[0], after), *chunks[1:], *weights, *gains],
            12,
            flops=2 * rows * width * 3 * cols,
        )
        if direct:
            spread = [kv] + [across(kv, d) for d in range(1, n_blk)]
        else:
            spread = {d: across(kv, d) if d else kv for d in (0, 1, *range(2, n_blk, 2))}
        queries.append(q)
        pieces.append(spread)
        groups.append(group)
        return q

    beside = {(1, 1): [fetch_first], (2, 1): [project], (3, 1): [project], (4, 1): [project]}
    fa, fb = own
    ba, bb = own
    waiting.append((0, *own))
    due = []
    for step in range(1, reach + 1):
        behind = fa
        fa = lax.ppermute(tied(fa, *due) if due else fa, "uly", ahead)
        bb = lax.ppermute(bb, "uly", back)
        due = [task(behind) for task in beside.get((step, 0), [])]
        if step < reach:
            behind = fb
            fb = lax.ppermute(tied(fb, *due) if due else fb, "uly", ahead)
            ba = lax.ppermute(ba, "uly", back)
            due = [task(behind) for task in beside.get((step, 1), [])]
            waiting += [(-step, fa, fb), (step, ba, bb)]
        else:
            due = [task(fb) for task in beside.get((step, 1), [])]
            waiting += [(reach, fa, bb)]
            project(fa, True)

    def second_leg(spread, after):
        for d in range(3, n_blk, 2):
            if isinstance(spread, dict):
                spread[d] = across(tied(spread[d - 1], after), 1)

    for spread in pieces[:-1]:
        second_leg(spread, queries[-1])
    sizes = [len(g) for g in groups]
    slots = [r for group in groups for r, *_ in group]
    total_rows = shard_rows * n_uly

    def some(sources, chosen):
        return [
            [
                (pieces[g][d], sizes[g] * (shard_rows if d < parts else video_rows))
                for d in sources[i : i + 2]
                for g in chosen
            ]
            for i in range(0, len(sources), 2)
        ]

    def attended(blocks, given, queries, kernel, outs, extra=(), more=0):
        counts = [[n for _, n in block] for block in blocks]
        keys = [piece for block in blocks for piece, _ in block]
        return call(
            functools.partial(kernel, counts, *queries),
            outs,
            [*given, *keys, *extra],
            16,
            flops=4 * total_rows * sum(map(sum, counts)) * cols + more,
        )

    state = [
        jax.ShapeDtypeStruct((2 * cols // HD, total_rows), F32),
        jax.ShapeDtypeStruct((cols, total_rows), F32),
    ]
    first = range(len(groups) - 1)
    outer = range(2, n_blk)
    query, *carried = attended(
        some((0, 1), first),
        queries,
        (len(queries),),
        attend_kernel,
        [jax.ShapeDtypeStruct((total_rows, cols), BF16), *state],
    )
    carried = attended(some(outer, first[:-1]), [query, *carried], (0,), attend_kernel, state)
    lead = width // 3
    left_rows = video_rows + text_rows * (width // lead)
    shapes = [
        jax.ShapeDtypeStruct((left_rows, lead), BF16),
        jax.ShapeDtypeStruct((video_rows, width - lead), BF16),
    ]
    last = [piece for block in some(outer, first[-1:]) + some(range(n_blk), (len(groups) - 1,)) for piece in block]
    video_heads, *lefts = attended(
        [last],
        [query, *carried],
        (sizes, video_rows),
        finish_kernel,
        [jax.ShapeDtypeStruct((video_rows * n_uly, cols), BF16)] + [shapes[0]] * n_uly,
        (video_output, text_output),
        2 * total_rows * cols * width,
    )
    rights = call(
        right_kernel,
        [shapes[1]] * n_uly,
        [video_heads, video_output],
        16,
        flops=2 * video_rows * n_uly * cols * (width - lead),
    )
    mine = {r: pair for r, *pair in zip(slots, lefts, rights)}
    mine[-reach] = mine[reach]

    def joined(arriving, own_part):
        return (arriving.astype(F32) + own_part.astype(F32)).astype(BF16)

    fa, bb = mine[reach][0], mine[-reach][1]
    fb, ba = mine[reach - 1][1], mine[1 - reach][0]
    for left in range(reach - 1, -1, -1):
        fa = lax.ppermute(fa, "uly", ahead)
        bb = lax.ppermute(bb, "uly", back)
        if left:
            fa = joined(fa, mine[left][0])
            bb = joined(bb, mine[-left][1])
            fb = lax.ppermute(fb, "uly", ahead)
            ba = lax.ppermute(ba, "uly", back)
            if left > 1:
                fb = joined(fb, mine[left - 1][1])
                ba = joined(ba, mine[1 - left][0])
    text_part = call(
        close_text_kernel,
        jax.ShapeDtypeStruct((text_rows, width), BF16),
        (fa, ba, mine[0][0], text_modulation),
        4,
    )
    pieces = [text_part] + [across(text_part, d) for d in range(1, parts)]
    return tuple(
        call(
            close_kernel,
            [jax.ShapeDtypeStruct(t.shape, BF16) for t in (video_tokens, text_tokens)],
            (part, fa, ba, mine[0][0], fb, bb, mine[0][1], video_modulation, *pieces),
            8,
            [pltpu.VMEM(text_tokens.shape, F32)],
            smem=(0,),
        )
    )


def solution(mesh):
    placed = (
        P(("blk", "uly"), None),
        P("uly", None),
        P(),
        P(),
        P(None, None, "uly"),
        P(None, None, "uly"),
        P("uly", None),
        P("uly", None),
        P(),
        P(),
    )
    return jax.shard_map(
        local,
        mesh=mesh,
        in_specs=placed,
        out_specs=(P(("blk", "uly"), None), P("uly", None)),
        check_vma=False,
    )
```

```python
import functools
import math

import jax
import jax.numpy as jnp
from jax import lax
from jax.experimental import pallas as pl
from jax.experimental.pallas import tpu as pltpu
from jax.sharding import PartitionSpec as P

HD = 128
EPS_NORM = 1e-06
F32 = jnp.float32
BF16 = jnp.bfloat16
VMEM = pl.BlockSpec(memory_space=pltpu.VMEM)
HBM = pl.BlockSpec(memory_space=pltpu.HBM)
SMEM = pl.BlockSpec(memory_space=pltpu.SMEM)


def call(kernel, outs, args, vmem_mib, scratch=(), flops=0, smem=(), hbm=()):
    moved = sum(a.size * a.dtype.itemsize for a in args)
    args = [pltpu.with_memory_space_constraint(a, pltpu.HBM) if i in hbm else a for i, a in enumerate(args)]
    return pl.pallas_call(
        kernel,
        out_shape=outs,
        in_specs=[SMEM if i in smem else HBM if i in hbm else VMEM for i in range(len(args))],
        out_specs=jax.tree.map(lambda _: VMEM, outs),
        scratch_shapes=list(scratch),
        compiler_params=pltpu.CompilerParams(vmem_limit_bytes=vmem_mib << 20),
        cost_estimate=pl.CostEstimate(flops=flops, bytes_accessed=moved, transcendentals=0),
    )(*args)


def ring_routes(axis):
    n = lax.axis_size(axis)
    order = list(range(0, n, 2)) + list(range(1, n, 2))[::-1]
    ahead = [(order[i], order[(i + 1) % n]) for i in range(n)]
    return ahead, [(b, a) for a, b in ahead]


def across(block, distance):
    n = lax.axis_size("blk")
    return lax.ppermute(block, "blk", [(i, i ^ distance) for i in range(n)])


def tied(block, *others):
    return lax.optimization_barrier((block, *others))[0]


def modulated(rows, factors):
    floats = rows.astype(F32)
    centre = floats - jnp.mean(floats, axis=-1, keepdims=True)
    spread = jnp.mean(centre * centre, axis=-1, keepdims=True)
    wide = factors.astype(F32)
    normed = centre / jnp.sqrt(spread + EPS_NORM)
    return normed * (1.0 + wide[1:2]) + wide[0:1]


def modulate_kernel(part_ref, *refs):
    sources, (left_ref, right_ref), landed = refs[:4], refs[4:6], refs[6:10]
    text_f32, sems = refs[10:]
    copies = [pltpu.make_async_copy(s, d, sems.at[i]) for i, (s, d) in enumerate(zip(sources, landed))]
    for copy in copies:
        copy.start()
    for copy in copies:
        copy.wait()
    video_ref, text_ref, vmod_ref, tmod_ref = landed
    text_rows = left_ref.shape[0] - video_ref.shape[0]
    half = left_ref.shape[1]
    text_f32[...] = text_ref[...].astype(F32)
    start = pl.multiple_of(part_ref[0] * text_rows, text_rows)
    own_text = text_f32[pl.ds(start, text_rows), :]
    video = modulated(video_ref[...], vmod_ref[...])
    text = modulated(own_text, tmod_ref[...])
    both = jnp.concatenate([video, text], axis=0).astype(BF16)
    left_ref[...] = both[:, :half]
    right_ref[...] = both[:, half:]


def bands(array, count):
    step = array.shape[-2] // count
    return [array.at[..., i * step : (i + 1) * step, :] for i in range(count)]


def fetch_kernel(counts, *refs):
    many = len(counts)
    copies = []
    for source, landed, count in zip(refs[:many], refs[many : 2 * many], counts):
        for pair in zip(bands(source, count), bands(landed, count)):
            copies.append(pltpu.make_async_copy(*pair, refs[-1].at[len(copies)]))
    for copy in copies:
        copy.start()
    for copy in copies:
        copy.wait()


def head_normed(mixture, gain):
    heads = []
    for h in range(mixture.shape[1] // HD):
        vectors = mixture[:, h * HD : (h + 1) * HD]
        inverse = lax.rsqrt(jnp.mean(vectors * vectors, axis=-1, keepdims=True) + EPS_NORM)
        heads.append(vectors * inverse * gain)
    return jnp.concatenate(heads, axis=1)


def project_kernel(shards, video_rows, *refs):
    chunks = refs[: 2 * shards]
    wv_ref, wt_ref, vgain_ref, tgain_ref, q_ref, kv_ref = refs[2 * shards :]
    width = q_ref.shape[1]
    video, text = [], []
    for side in range(2):
        floats = [chunks[2 * i + side][...].astype(F32) for i in range(shards)]
        video.append(jnp.concatenate([f[:video_rows] for f in floats], axis=0).astype(BF16))
        text.append(jnp.concatenate([f[video_rows:] for f in floats], axis=0).astype(BF16))
    half = video[0].shape[1]

    def mixed(sides, w_ref, j):
        total = jnp.dot(sides[0], w_ref[j, :half, :], preferred_element_type=F32)
        return total + jnp.dot(sides[1], w_ref[j, half:, :], preferred_element_type=F32)

    def joined(j, norm):
        v = mixed(video, wv_ref, j)
        t = mixed(text, wt_ref, j)
        if norm:
            v = head_normed(v, vgain_ref[j : j + 1, :])
            t = head_normed(t, tgain_ref[j : j + 1, :])
        return jnp.concatenate([v, t], axis=0).astype(BF16)

    q_ref[...] = joined(0, True)
    kv_ref[:, :width] = joined(1, True)
    kv_ref[:, width:] = joined(2, False)


def wide_rows(refs, counts):
    return jnp.concatenate([r[...].astype(F32)[:n] for r, n in zip(refs, counts)], axis=0).astype(BF16)


def absorbed(state, query, block):
    width = query.shape[1]
    factor = HD ** (-0.5) * math.log2(math.e)
    raised = []
    for h in range(width // HD):
        mine = slice(h * HD, (h + 1) * HD)
        scores = lax.dot_general(
            block[:, mine], query[:, mine], (((1,), (1,)), ((), ())), preferred_element_type=F32
        )
        highest = jnp.max(scores, axis=0, keepdims=True)
        if state:
            before, totals, sums = state[h]
            highest = jnp.maximum(before, highest)
        weights = jnp.exp2((scores - highest) * factor)
        total = jnp.sum(weights, axis=0, keepdims=True)
        mixed = lax.dot_general(
            block[:, width + h * HD : width + (h + 1) * HD],
            weights.astype(BF16),
            (((0,), (0,)), ((), ())),
            preferred_element_type=F32,
        )
        if state:
            shrink = jnp.exp2((before - highest) * factor)
            total = totals * shrink + total
            mixed = sums * shrink + mixed
        raised.append((highest, total, mixed))
    return raised


def load_state(stats_ref, sums_ref):
    heads = stats_ref.shape[0] // 2
    return [
        (
            stats_ref[h : h + 1, :],
            stats_ref[heads + h : heads + h + 1, :],
            sums_ref[h * HD : (h + 1) * HD, :],
        )
        for h in range(heads)
    ]


def absorb_blocks(state, query, blocks, pieces):
    start = 0
    for counts in blocks:
        held = pieces[start : start + len(counts)]
        state = absorbed(state, query, wide_rows(held, counts))
        start += len(counts)
    return state


def attend_kernel(blocks, queries, *refs):
    if queries:
        query = wide_rows(refs[:queries], [r.shape[0] for r in refs[:queries]])
        pieces, (query_ref, stats_ref, sums_ref) = refs[queries:-3], refs[-3:]
        query_ref[...] = query
        state = absorb_blocks([], query, blocks, pieces)
    else:
        query, state = refs[0][...], load_state(*refs[1:3])
        pieces, (stats_ref, sums_ref) = refs[3:-2], refs[-2:]
        state = absorb_blocks(state, query, blocks, pieces)
    heads = len(state)
    for h, (highest, totals, sums) in enumerate(state):
        stats_ref[h : h + 1, :] = highest
        stats_ref[heads + h : heads + h + 1, :] = totals
        sums_ref[h * HD : (h + 1) * HD, :] = sums


def finish_kernel(blocks, sizes, video_rows, query_ref, stats_ref, sums_ref, *refs):
    held = sum(len(counts) for counts in blocks)
    pieces, weights, outs = refs[:held], refs[held : held + 2], refs[held + 2 :]
    state = absorb_blocks(load_state(stats_ref, sums_ref), query_ref[...], blocks, pieces)
    flat = jnp.concatenate([sums / totals for _, totals, sums in state], axis=0)
    rows_out = jnp.transpose(flat)
    text_rows = rows_out.shape[0] // sum(sizes) - video_rows
    video, text = [], []
    start = 0
    for size in sizes:
        video.append(rows_out[start : start + size * video_rows])
        start += size * video_rows
        text.append(rows_out[start : start + size * text_rows])
        start += size * text_rows
    video, text = [jnp.concatenate(rows, axis=0).astype(BF16) for rows in (video, text)]
    video_ref, *outs = outs
    video_ref[...] = video
    lead = outs[0].shape[1]
    left = jnp.dot(video, weights[0][:, :lead], preferred_element_type=F32)
    bands = [
        jnp.dot(text, weights[1][:, c : c + lead], preferred_element_type=F32)
        for c in range(0, weights[1].shape[1], lead)
    ]
    for i, out in enumerate(outs):
        rows = [left[i * video_rows : (i + 1) * video_rows]]
        rows += [y[i * text_rows : (i + 1) * text_rows] for y in bands]
        out[...] = jnp.concatenate(rows, axis=0).astype(BF16)


def right_kernel(video_ref, wv_ref, *outs):
    video_rows, columns = outs[0].shape
    lead = wv_ref.shape[1] - columns
    right = jnp.dot(video_ref[...], wv_ref[:, lead:], preferred_element_type=F32)
    for i, out in enumerate(outs):
        out[...] = right[i * video_rows : (i + 1) * video_rows].astype(BF16)


def close_text_kernel(fa_ref, ba_ref, own_ref, tmod_ref, text_ref):
    text_rows, width = text_ref.shape
    lead = own_ref.shape[1]
    start = own_ref.shape[0] - text_rows * (width // lead)
    total = sum(r[...].astype(F32)[start:] for r in (fa_ref, ba_ref, own_ref))
    for band in range(width // lead):
        columns = slice(band * lead, (band + 1) * lead)
        gate = tmod_ref[2:3, columns].astype(F32)
        text_ref[:, columns] = (total[band * text_rows : (band + 1) * text_rows] * gate).astype(BF16)


def close_kernel(part_ref, fa, ba, own_a, fb, bb, own_b, vmod_ref, *refs):
    pieces, (video_ref, text_ref, wide) = refs[:-3], refs[-3:]
    video_rows, width = video_ref.shape
    lead = own_a.shape[1]
    for columns, arrivals in ((slice(0, lead), (fa, ba, own_a)), (slice(lead, width), (fb, bb, own_b))):
        total = sum(r[...].astype(F32)[:video_rows] for r in arrivals)
        video_ref[:, columns] = (total * vmod_ref[2:3, columns].astype(F32)).astype(BF16)
    rows = pieces[0].shape[0]
    for d, piece in enumerate(pieces):
        start = pl.multiple_of((part_ref[0] ^ d) * rows, rows)
        wide[pl.ds(start, rows), :] = piece[...].astype(F32)
    text_ref[...] = wide[...].astype(BF16)


def local(
    video_tokens,
    text_tokens,
    video_modulation,
    text_modulation,
    video_projection,
    text_projection,
    video_output,
    text_output,
    video_gains,
    text_gains,
):
    n_blk, n_uly = lax.axis_size("blk"), lax.axis_size("uly")
    reach = n_uly // 2
    ahead, back = ring_routes("uly")
    video_rows, width = video_tokens.shape
    half = width // 2
    parts = math.gcd(n_blk, text_tokens.shape[0] // 8)
    text_rows = text_tokens.shape[0] // parts
    shard_rows = video_rows + text_rows
    cols = video_output.shape[0]
    part = lax.rem(lax.axis_index("blk"), parts).reshape(1).astype(jnp.int32)

    chunk = jax.ShapeDtypeStruct((shard_rows, half), BF16)
    own = call(
        modulate_kernel,
        [chunk, chunk],
        (part, video_tokens, text_tokens, video_modulation, text_modulation),
        8,
        [pltpu.VMEM(a.shape, BF16) for a in (video_tokens, text_tokens, video_modulation, text_modulation)]
        + [pltpu.VMEM(text_tokens.shape, F32), pltpu.SemaphoreType.DMA((4,))],
        smem=(0,),
        hbm=(1, 2, 3, 4),
    )

    def fetched(arrays, counts, after):
        arrays = [tied(arrays[0], after), *arrays[1:]]
        return call(
            functools.partial(fetch_kernel, counts),
            [jax.ShapeDtypeStruct(a.shape, a.dtype) for a in arrays],
            arrays,
            1,
            [pltpu.SemaphoreType.DMA((sum(counts),))],
            hbm=range(len(arrays)),
        )

    weights, gains = [], []
    waiting = []
    queries, pieces, groups = [], [], []

    def fetch_first(after):
        held = [jnp.transpose(p, (1, 0, 2)) for p in (video_projection, text_projection)]
        *held, vgains, tgains = fetched([*held, video_gains, text_gains], [4, 4, 1, 1], after)
        weights.extend(held)
        gains.extend((vgains, tgains))
        return held[0]

    def project(after, direct=False):
        group = list(waiting)
        waiting.clear()
        rows = len(group) * shard_rows
        chunks = [c for _, *pair in group for c in pair]
        q, kv = call(
            functools.partial(project_kernel, len(group), video_rows),
            [
                jax.ShapeDtypeStruct((rows, cols), BF16),
                jax.ShapeDtypeStruct((rows, 2 * cols), BF16),
            ],
            [tied(chunks[0], after), *chunks[1:], *weights, *gains],
            12,
            flops=2 * rows * width * 3 * cols,
        )
        if direct:
            spread = [kv] + [across(kv, d) for d in range(1, n_blk)]
        else:
            spread = {d: across(kv, d) if d else kv for d in (0, 1, *range(2, n_blk, 2))}
        queries.append(q)
        pieces.append(spread)
        groups.append(group)
        return q

    beside = {(1, 1): [fetch_first], (2, 1): [project], (3, 1): [project], (4, 1): [project]}
    fa, fb = own
    ba, bb = own
    waiting.append((0, *own))
    due = []
    for step in range(1, reach + 1):
        behind = fa
        fa = lax.ppermute(tied(fa, *due) if due else fa, "uly", ahead)
        bb = lax.ppermute(bb, "uly", back)
        due = [task(behind) for task in beside.get((step, 0), [])]
        if step < reach:
            behind = fb
            fb = lax.ppermute(tied(fb, *due) if due else fb, "uly", ahead)
            ba = lax.ppermute(ba, "uly", back)
            due = [task(behind) for task in beside.get((step, 1), [])]
            waiting += [(-step, fa, fb), (step, ba, bb)]
        else:
            due = [task(fb) for task in beside.get((step, 1), [])]
            waiting += [(reach, fa, bb)]
            project(fa, True)

    def second_leg(spread, after):
        for d in range(3, n_blk, 2):
            if isinstance(spread, dict):
                spread[d] = across(tied(spread[d - 1], after), 1)

    for spread in pieces[:-1]:
        second_leg(spread, queries[-1])
    sizes = [len(g) for g in groups]
    slots = [r for group in groups for r, *_ in group]
    total_rows = shard_rows * n_uly

    def some(sources, chosen):
        return [
            [
                (pieces[g][d], sizes[g] * (shard_rows if d < parts else video_rows))
                for d in sources[i : i + 2]
                for g in chosen
            ]
            for i in range(0, len(sources), 2)
        ]

    def attended(blocks, given, queries, kernel, outs, extra=(), more=0):
        counts = [[n for _, n in block] for block in blocks]
        keys = [piece for block in blocks for piece, _ in block]
        return call(
            functools.partial(kernel, counts, *queries),
            outs,
            [*given, *keys, *extra],
            16,
            flops=4 * total_rows * sum(map(sum, counts)) * cols + more,
        )

    state = [
        jax.ShapeDtypeStruct((2 * cols // HD, total_rows), F32),
        jax.ShapeDtypeStruct((cols, total_rows), F32),
    ]
    first = range(len(groups) - 1)
    outer = range(2, n_blk)
    query, *carried = attended(
        some((0, 1), first) + some(outer, first[:-1]),
        queries,
        (len(queries),),
        attend_kernel,
        [jax.ShapeDtypeStruct((total_rows, cols), BF16), *state],
    )
    lead = width // 3
    left_rows = video_rows + text_rows * (width // lead)
    shapes = [
        jax.ShapeDtypeStruct((left_rows, lead), BF16),
        jax.ShapeDtypeStruct((video_rows, width - lead), BF16),
    ]
    last = [piece for block in some(outer, first[-1:]) + some(range(n_blk), (len(groups) - 1,)) for piece in block]
    video_heads, *lefts = attended(
        [last],
        [query, *carried],
        (sizes, video_rows),
        finish_kernel,
        [jax.ShapeDtypeStruct((video_rows * n_uly, cols), BF16)] + [shapes[0]] * n_uly,
        (video_output, text_output),
        2 * total_rows * cols * width,
    )
    rights = call(
        right_kernel,
        [shapes[1]] * n_uly,
        [video_heads, video_output],
        16,
        flops=2 * video_rows * n_uly * cols * (width - lead),
    )
    mine = {r: pair for r, *pair in zip(slots, lefts, rights)}
    mine[-reach] = mine[reach]

    def joined(arriving, own_part):
        return (arriving.astype(F32) + own_part.astype(F32)).astype(BF16)

    fa, bb = mine[reach][0], mine[-reach][1]
    fb, ba = mine[reach - 1][1], mine[1 - reach][0]
    for left in range(reach - 1, -1, -1):
        fa = lax.ppermute(fa, "uly", ahead)
        bb = lax.ppermute(bb, "uly", back)
        if left:
            fa = joined(fa, mine[left][0])
            bb = joined(bb, mine[-left][1])
            fb = lax.ppermute(fb, "uly", ahead)
            ba = lax.ppermute(ba, "uly", back)
            if left > 1:
                fb = joined(fb, mine[left - 1][1])
                ba = joined(ba, mine[1 - left][0])
    text_part = call(
        close_text_kernel,
        jax.ShapeDtypeStruct((text_rows, width), BF16),
        (fa, ba, mine[0][0], text_modulation),
        4,
    )
    pieces = [text_part] + [across(text_part, d) for d in range(1, parts)]
    return tuple(
        call(
            close_kernel,
            [jax.ShapeDtypeStruct(t.shape, BF16) for t in (video_tokens, text_tokens)],
            (part, fa, ba, mine[0][0], fb, bb, mine[0][1], video_modulation, *pieces),
            8,
            [pltpu.VMEM(text_tokens.shape, F32)],
            smem=(0,),
        )
    )


def solution(mesh):
    placed = (
        P(("blk", "uly"), None),
        P("uly", None),
        P(),
        P(),
        P(None, None, "uly"),
        P(None, None, "uly"),
        P("uly", None),
        P("uly", None),
        P(),
        P(),
    )
    return jax.shard_map(
        local,
        mesh=mesh,
        in_specs=placed,
        out_specs=(P(("blk", "uly"), None), P("uly", None)),
        check_vma=False,
    )
```

```python
import functools
import math

import jax
import jax.numpy as jnp
from jax import lax
from jax.experimental import pallas as pl
from jax.experimental.pallas import tpu as pltpu
from jax.sharding import PartitionSpec as P

HD = 128
EPS_NORM = 1e-06
F32 = jnp.float32
BF16 = jnp.bfloat16
VMEM = pl.BlockSpec(memory_space=pltpu.VMEM)
HBM = pl.BlockSpec(memory_space=pltpu.HBM)
SMEM = pl.BlockSpec(memory_space=pltpu.SMEM)


def call(kernel, outs, args, vmem_mib, scratch=(), flops=0, smem=(), hbm=()):
    moved = sum(a.size * a.dtype.itemsize for a in args)
    args = [pltpu.with_memory_space_constraint(a, pltpu.HBM) if i in hbm else a for i, a in enumerate(args)]
    return pl.pallas_call(
        kernel,
        out_shape=outs,
        in_specs=[SMEM if i in smem else HBM if i in hbm else VMEM for i in range(len(args))],
        out_specs=jax.tree.map(lambda _: VMEM, outs),
        scratch_shapes=list(scratch),
        compiler_params=pltpu.CompilerParams(vmem_limit_bytes=vmem_mib << 20),
        cost_estimate=pl.CostEstimate(flops=flops, bytes_accessed=moved, transcendentals=0),
    )(*args)


def ring_routes(axis):
    n = lax.axis_size(axis)
    order = list(range(0, n, 2)) + list(range(1, n, 2))[::-1]
    ahead = [(order[i], order[(i + 1) % n]) for i in range(n)]
    return ahead, [(b, a) for a, b in ahead]


def across(block, distance):
    n = lax.axis_size("blk")
    return lax.ppermute(block, "blk", [(i, i ^ distance) for i in range(n)])


def tied(block, *others):
    return lax.optimization_barrier((block, *others))[0]


def modulated(rows, factors):
    floats = rows.astype(F32)
    centre = floats - jnp.mean(floats, axis=-1, keepdims=True)
    spread = jnp.mean(centre * centre, axis=-1, keepdims=True)
    wide = factors.astype(F32)
    normed = centre / jnp.sqrt(spread + EPS_NORM)
    return normed * (1.0 + wide[1:2]) + wide[0:1]


def modulate_kernel(part_ref, *refs):
    sources, (left_ref, right_ref), landed = refs[:4], refs[4:6], refs[6:10]
    text_f32, sems = refs[10:]
    copies = [pltpu.make_async_copy(s, d, sems.at[i]) for i, (s, d) in enumerate(zip(sources, landed))]
    for copy in copies:
        copy.start()
    for copy in copies:
        copy.wait()
    video_ref, text_ref, vmod_ref, tmod_ref = landed
    text_rows = left_ref.shape[0] - video_ref.shape[0]
    half = left_ref.shape[1]
    text_f32[...] = text_ref[...].astype(F32)
    start = pl.multiple_of(part_ref[0] * text_rows, text_rows)
    own_text = text_f32[pl.ds(start, text_rows), :]
    video = modulated(video_ref[...], vmod_ref[...])
    text = modulated(own_text, tmod_ref[...])
    both = jnp.concatenate([video, text], axis=0).astype(BF16)
    left_ref[...] = both[:, :half]
    right_ref[...] = both[:, half:]


def bands(array, count):
    step = array.shape[-2] // count
    return [array.at[..., i * step : (i + 1) * step, :] for i in range(count)]


def fetch_kernel(counts, *refs):
    many = len(counts)
    copies = []
    for source, landed, count in zip(refs[:many], refs[many : 2 * many], counts):
        for pair in zip(bands(source, count), bands(landed, count)):
            copies.append(pltpu.make_async_copy(*pair, refs[-1].at[len(copies)]))
    for copy in copies:
        copy.start()
    for copy in copies:
        copy.wait()


def head_normed(mixture, gain):
    heads = []
    for h in range(mixture.shape[1] // HD):
        vectors = mixture[:, h * HD : (h + 1) * HD]
        inverse = lax.rsqrt(jnp.mean(vectors * vectors, axis=-1, keepdims=True) + EPS_NORM)
        heads.append(vectors * inverse * gain)
    return jnp.concatenate(heads, axis=1)


def project_kernel(shards, video_rows, *refs):
    chunks = refs[: 2 * shards]
    wv_ref, wt_ref, vgain_ref, tgain_ref, q_ref, kv_ref = refs[2 * shards :]
    width = q_ref.shape[1]
    video, text = [], []
    for side in range(2):
        mine = [chunks[2 * i + side] for i in range(shards)]
        video.append(jnp.concatenate([r[:video_rows, :] for r in mine], axis=0))
        text.append(jnp.concatenate([r[...].astype(F32)[video_rows:] for r in mine], axis=0).astype(BF16))
    half = video[0].shape[1]

    def mixed(sides, w_ref, j):
        total = jnp.dot(sides[0], w_ref[j, :half, :], preferred_element_type=F32)
        return total + jnp.dot(sides[1], w_ref[j, half:, :], preferred_element_type=F32)

    def joined(j, norm):
        v = mixed(video, wv_ref, j)
        t = mixed(text, wt_ref, j)
        if norm:
            v = head_normed(v, vgain_ref[j : j + 1, :])
            t = head_normed(t, tgain_ref[j : j + 1, :])
        return jnp.concatenate([v, t], axis=0).astype(BF16)

    q_ref[...] = joined(0, True)
    kv_ref[:, :width] = joined(1, True)
    kv_ref[:, width:] = joined(2, False)


def wide_rows(refs, counts):
    return jnp.concatenate([r[...].astype(F32)[:n] for r, n in zip(refs, counts)], axis=0).astype(BF16)


def absorbed(state, query, block):
    width = query.shape[1]
    factor = HD ** (-0.5) * math.log2(math.e)
    raised = []
    for h in range(width // HD):
        mine = slice(h * HD, (h + 1) * HD)
        scores = lax.dot_general(
            block[:, mine], query[:, mine], (((1,), (1,)), ((), ())), preferred_element_type=F32
        )
        highest = jnp.max(scores, axis=0, keepdims=True)
        if state:
            before, totals, sums = state[h]
            highest = jnp.maximum(before, highest)
        weights = jnp.exp2((scores - highest) * factor)
        total = jnp.sum(weights, axis=0, keepdims=True)
        mixed = lax.dot_general(
            block[:, width + h * HD : width + (h + 1) * HD],
            weights.astype(BF16),
            (((0,), (0,)), ((), ())),
            preferred_element_type=F32,
        )
        if state:
            shrink = jnp.exp2((before - highest) * factor)
            total = totals * shrink + total
            mixed = sums * shrink + mixed
        raised.append((highest, total, mixed))
    return raised


def load_state(stats_ref, sums_ref):
    heads = stats_ref.shape[0] // 2
    return [
        (
            stats_ref[h : h + 1, :],
            stats_ref[heads + h : heads + h + 1, :],
            sums_ref[h * HD : (h + 1) * HD, :],
        )
        for h in range(heads)
    ]


def absorb_blocks(state, query, blocks, pieces):
    start = 0
    for counts in blocks:
        held = pieces[start : start + len(counts)]
        state = absorbed(state, query, wide_rows(held, counts))
        start += len(counts)
    return state


def attend_kernel(blocks, queries, *refs):
    if queries:
        query = wide_rows(refs[:queries], [r.shape[0] for r in refs[:queries]])
        pieces, (query_ref, stats_ref, sums_ref) = refs[queries:-3], refs[-3:]
        query_ref[...] = query
        state = absorb_blocks([], query, blocks, pieces)
    else:
        query, state = refs[0][...], load_state(*refs[1:3])
        pieces, (stats_ref, sums_ref) = refs[3:-2], refs[-2:]
        state = absorb_blocks(state, query, blocks, pieces)
    heads = len(state)
    for h, (highest, totals, sums) in enumerate(state):
        stats_ref[h : h + 1, :] = highest
        stats_ref[heads + h : heads + h + 1, :] = totals
        sums_ref[h * HD : (h + 1) * HD, :] = sums


def finish_kernel(blocks, sizes, video_rows, query_ref, stats_ref, sums_ref, *refs):
    held = sum(len(counts) for counts in blocks)
    pieces, weights, outs = refs[:held], refs[held : held + 2], refs[held + 2 :]
    state = absorb_blocks(load_state(stats_ref, sums_ref), query_ref[...], blocks, pieces)
    flat = jnp.concatenate([sums / totals for _, totals, sums in state], axis=0)
    rows_out = jnp.transpose(flat)
    text_rows = rows_out.shape[0] // sum(sizes) - video_rows
    video, text = [], []
    start = 0
    for size in sizes:
        video.append(rows_out[start : start + size * video_rows])
        start += size * video_rows
        text.append(rows_out[start : start + size * text_rows])
        start += size * text_rows
    video, text = [jnp.concatenate(rows, axis=0).astype(BF16) for rows in (video, text)]
    video_ref, *outs = outs
    video_ref[...] = video
    lead = outs[0].shape[1]
    left = jnp.dot(video, weights[0][:, :lead], preferred_element_type=F32)
    bands = [
        jnp.dot(text, weights[1][:, c : c + lead], preferred_element_type=F32)
        for c in range(0, weights[1].shape[1], lead)
    ]
    for i, out in enumerate(outs):
        rows = [left[i * video_rows : (i + 1) * video_rows]]
        rows += [y[i * text_rows : (i + 1) * text_rows] for y in bands]
        out[...] = jnp.concatenate(rows, axis=0).astype(BF16)


def right_kernel(video_ref, wv_ref, *outs):
    video_rows, columns = outs[0].shape
    lead = wv_ref.shape[1] - columns
    right = jnp.dot(video_ref[...], wv_ref[:, lead:], preferred_element_type=F32)
    for i, out in enumerate(outs):
        out[...] = right[i * video_rows : (i + 1) * video_rows].astype(BF16)


def close_text_kernel(fa_ref, ba_ref, own_ref, tmod_ref, text_ref):
    text_rows, width = text_ref.shape
    lead = own_ref.shape[1]
    start = own_ref.shape[0] - text_rows * (width // lead)
    total = sum(r[...].astype(F32)[start:] for r in (fa_ref, ba_ref, own_ref))
    for band in range(width // lead):
        columns = slice(band * lead, (band + 1) * lead)
        gate = tmod_ref[2:3, columns].astype(F32)
        text_ref[:, columns] = (total[band * text_rows : (band + 1) * text_rows] * gate).astype(BF16)


def close_kernel(part_ref, fa, ba, own_a, fb, bb, own_b, vmod_ref, *refs):
    pieces, (video_ref, text_ref, wide) = refs[:-3], refs[-3:]
    video_rows, width = video_ref.shape
    lead = own_a.shape[1]
    for columns, arrivals in ((slice(0, lead), (fa, ba, own_a)), (slice(lead, width), (fb, bb, own_b))):
        total = sum(r[...].astype(F32)[:video_rows] for r in arrivals)
        video_ref[:, columns] = (total * vmod_ref[2:3, columns].astype(F32)).astype(BF16)
    rows = pieces[0].shape[0]
    for d, piece in enumerate(pieces):
        start = pl.multiple_of((part_ref[0] ^ d) * rows, rows)
        wide[pl.ds(start, rows), :] = piece[...].astype(F32)
    text_ref[...] = wide[...].astype(BF16)


def local(
    video_tokens,
    text_tokens,
    video_modulation,
    text_modulation,
    video_projection,
    text_projection,
    video_output,
    text_output,
    video_gains,
    text_gains,
):
    n_blk, n_uly = lax.axis_size("blk"), lax.axis_size("uly")
    reach = n_uly // 2
    ahead, back = ring_routes("uly")
    video_rows, width = video_tokens.shape
    half = width // 2
    parts = math.gcd(n_blk, text_tokens.shape[0] // 8)
    text_rows = text_tokens.shape[0] // parts
    shard_rows = video_rows + text_rows
    cols = video_output.shape[0]
    part = lax.rem(lax.axis_index("blk"), parts).reshape(1).astype(jnp.int32)

    chunk = jax.ShapeDtypeStruct((shard_rows, half), BF16)
    own = call(
        modulate_kernel,
        [chunk, chunk],
        (part, video_tokens, text_tokens, video_modulation, text_modulation),
        8,
        [pltpu.VMEM(a.shape, BF16) for a in (video_tokens, text_tokens, video_modulation, text_modulation)]
        + [pltpu.VMEM(text_tokens.shape, F32), pltpu.SemaphoreType.DMA((4,))],
        smem=(0,),
        hbm=(1, 2, 3, 4),
    )

    def fetched(arrays, counts, after):
        arrays = [tied(arrays[0], after), *arrays[1:]]
        return call(
            functools.partial(fetch_kernel, counts),
            [jax.ShapeDtypeStruct(a.shape, a.dtype) for a in arrays],
            arrays,
            1,
            [pltpu.SemaphoreType.DMA((sum(counts),))],
            hbm=range(len(arrays)),
        )

    weights, gains, ends = [], [], []
    waiting = []
    queries, pieces, groups = [], [], []

    def fetch_first(after):
        held = [jnp.transpose(p, (1, 0, 2)) for p in (video_projection, text_projection)]
        *held, vgains, tgains = fetched([*held, video_gains, text_gains], [4, 4, 1, 1], after)
        weights.extend(held)
        gains.extend((vgains, tgains))
        return held[0]

    def fetch_last(after):
        ends.extend(fetched([video_output, text_output], [2, 2], after))
        return ends[0]

    def project(after, direct=False):
        group = list(waiting)
        waiting.clear()
        rows = len(group) * shard_rows
        chunks = [c for _, *pair in group for c in pair]
        q, kv = call(
            functools.partial(project_kernel, len(group), video_rows),
            [
                jax.ShapeDtypeStruct((rows, cols), BF16),
                jax.ShapeDtypeStruct((rows, 2 * cols), BF16),
            ],
            [tied(chunks[0], after), *chunks[1:], *weights, *gains],
            12,
            flops=2 * rows * width * 3 * cols,
        )
        if direct:
            spread = [kv] + [across(kv, d) for d in range(1, n_blk)]
        else:
            spread = {d: across(kv, d) if d else kv for d in (0, 1, *range(2, n_blk, 2))}
        queries.append(q)
        pieces.append(spread)
        groups.append(group)
        return q

    beside = {(1, 1): [fetch_first], (2, 1): [project], (3, 1): [project], (4, 1): [project]}
    fa, fb = own
    ba, bb = own
    waiting.append((0, *own))
    due = []
    for step in range(1, reach + 1):
        behind = fa
        fa = lax.ppermute(tied(fa, *due) if due else fa, "uly", ahead)
        bb = lax.ppermute(bb, "uly", back)
        due = [task(behind) for task in beside.get((step, 0), [])]
        if step < reach:
            behind = fb
            fb = lax.ppermute(tied(fb, *due) if due else fb, "uly", ahead)
            ba = lax.ppermute(ba, "uly", back)
            due = [task(behind) for task in beside.get((step, 1), [])]
            waiting += [(-step, fa, fb), (step, ba, bb)]
        else:
            due = [task(fb) for task in beside.get((step, 1), [])]
            waiting += [(reach, fa, bb)]
            project(fa, True)

    def second_leg(spread, after):
        for d in range(3, n_blk, 2):
            if isinstance(spread, dict):
                spread[d] = across(tied(spread[d - 1], after), 1)

    for spread in pieces[:-1]:
        second_leg(spread, queries[-1])
    sizes = [len(g) for g in groups]
    slots = [r for group in groups for r, *_ in group]
    total_rows = shard_rows * n_uly

    def some(sources, chosen):
        return [
            [
                (pieces[g][d], sizes[g] * (shard_rows if d < parts else video_rows))
                for d in sources[i : i + 2]
                for g in chosen
            ]
            for i in range(0, len(sources), 2)
        ]

    def attended(blocks, given, queries, kernel, outs, extra=(), more=0):
        counts = [[n for _, n in block] for block in blocks]
        keys = [piece for block in blocks for piece, _ in block]
        return call(
            functools.partial(kernel, counts, *queries),
            outs,
            [*given, *keys, *extra],
            16,
            flops=4 * total_rows * sum(map(sum, counts)) * cols + more,
        )

    state = [
        jax.ShapeDtypeStruct((2 * cols // HD, total_rows), F32),
        jax.ShapeDtypeStruct((cols, total_rows), F32),
    ]
    first = range(len(groups) - 1)
    outer = range(2, n_blk)
    query, *carried = attended(
        some((0, 1), first),
        queries,
        (len(queries),),
        attend_kernel,
        [jax.ShapeDtypeStruct((total_rows, cols), BF16), *state],
    )
    carried = attended(some(outer, first[:-1]), [query, *carried], (0,), attend_kernel, state)
    lead = width // 3
    left_rows = video_rows + text_rows * (width // lead)
    shapes = [
        jax.ShapeDtypeStruct((left_rows, lead), BF16),
        jax.ShapeDtypeStruct((video_rows, width - lead), BF16),
    ]
    last = [piece for block in some(outer, first[-1:]) + some(range(n_blk), (len(groups) - 1,)) for piece in block]
    video_heads, *lefts = attended(
        [last],
        [query, *carried],
        (sizes, video_rows),
        finish_kernel,
        [jax.ShapeDtypeStruct((video_rows * n_uly, cols), BF16)] + [shapes[0]] * n_uly,
        (video_output, text_output),
        2 * total_rows * cols * width,
    )
    rights = call(
        right_kernel,
        [shapes[1]] * n_uly,
        [video_heads, video_output],
        16,
        flops=2 * video_rows * n_uly * cols * (width - lead),
    )
    mine = {r: pair for r, *pair in zip(slots, lefts, rights)}
    mine[-reach] = mine[reach]

    def joined(arriving, own_part):
        return (arriving.astype(F32) + own_part.astype(F32)).astype(BF16)

    fa, bb = mine[reach][0], mine[-reach][1]
    fb, ba = mine[reach - 1][1], mine[1 - reach][0]
    for left in range(reach - 1, -1, -1):
        fa = lax.ppermute(fa, "uly", ahead)
        bb = lax.ppermute(bb, "uly", back)
        if left:
            fa = joined(fa, mine[left][0])
            bb = joined(bb, mine[-left][1])
            fb = lax.ppermute(fb, "uly", ahead)
            ba = lax.ppermute(ba, "uly", back)
            if left > 1:
                fb = joined(fb, mine[left - 1][1])
                ba = joined(ba, mine[1 - left][0])
    text_part = call(
        close_text_kernel,
        jax.ShapeDtypeStruct((text_rows, width), BF16),
        (fa, ba, mine[0][0], text_modulation),
        4,
    )
    pieces = [text_part] + [across(text_part, d) for d in range(1, parts)]
    return tuple(
        call(
            close_kernel,
            [jax.ShapeDtypeStruct(t.shape, BF16) for t in (video_tokens, text_tokens)],
            (part, fa, ba, mine[0][0], fb, bb, mine[0][1], video_modulation, *pieces),
            8,
            [pltpu.VMEM(text_tokens.shape, F32)],
            smem=(0,),
        )
    )


def solution(mesh):
    placed = (
        P(("blk", "uly"), None),
        P("uly", None),
        P(),
        P(),
        P(None, None, "uly"),
        P(None, None, "uly"),
        P("uly", None),
        P("uly", None),
        P(),
        P(),
    )
    return jax.shard_map(
        local,
        mesh=mesh,
        in_specs=placed,
        out_specs=(P(("blk", "uly"), None), P("uly", None)),
        check_vma=False,
    )
```

```python
import functools
import math

import jax
import jax.numpy as jnp
from jax import lax
from jax.experimental import pallas as pl
from jax.experimental.pallas import tpu as pltpu
from jax.sharding import PartitionSpec as P

HD = 128
EPS_NORM = 1e-06
F32 = jnp.float32
BF16 = jnp.bfloat16
VMEM = pl.BlockSpec(memory_space=pltpu.VMEM)
HBM = pl.BlockSpec(memory_space=pltpu.HBM)
SMEM = pl.BlockSpec(memory_space=pltpu.SMEM)


def call(kernel, outs, args, vmem_mib, scratch=(), flops=0, smem=(), hbm=()):
    moved = sum(a.size * a.dtype.itemsize for a in args)
    args = [pltpu.with_memory_space_constraint(a, pltpu.HBM) if i in hbm else a for i, a in enumerate(args)]
    return pl.pallas_call(
        kernel,
        out_shape=outs,
        in_specs=[SMEM if i in smem else HBM if i in hbm else VMEM for i in range(len(args))],
        out_specs=jax.tree.map(lambda _: VMEM, outs),
        scratch_shapes=list(scratch),
        compiler_params=pltpu.CompilerParams(vmem_limit_bytes=vmem_mib << 20),
        cost_estimate=pl.CostEstimate(flops=flops, bytes_accessed=moved, transcendentals=0),
    )(*args)


def ring_routes(axis):
    n = lax.axis_size(axis)
    order = list(range(0, n, 2)) + list(range(1, n, 2))[::-1]
    ahead = [(order[i], order[(i + 1) % n]) for i in range(n)]
    return ahead, [(b, a) for a, b in ahead]


def across(block, distance):
    n = lax.axis_size("blk")
    return lax.ppermute(block, "blk", [(i, i ^ distance) for i in range(n)])


def tied(block, *others):
    return lax.optimization_barrier((block, *others))[0]


def modulated(rows, factors):
    floats = rows.astype(F32)
    centre = floats - jnp.mean(floats, axis=-1, keepdims=True)
    spread = jnp.mean(centre * centre, axis=-1, keepdims=True)
    wide = factors.astype(F32)
    normed = centre / jnp.sqrt(spread + EPS_NORM)
    return normed * (1.0 + wide[1:2]) + wide[0:1]


def modulate_kernel(part_ref, *refs):
    sources, (left_ref, right_ref), landed = refs[:4], refs[4:6], refs[6:10]
    text_f32, sems = refs[10:]
    copies = [pltpu.make_async_copy(s, d, sems.at[i]) for i, (s, d) in enumerate(zip(sources, landed))]
    for copy in copies:
        copy.start()
    for copy in copies:
        copy.wait()
    video_ref, text_ref, vmod_ref, tmod_ref = landed
    text_rows = left_ref.shape[0] - video_ref.shape[0]
    half = left_ref.shape[1]
    text_f32[...] = text_ref[...].astype(F32)
    start = pl.multiple_of(part_ref[0] * text_rows, text_rows)
    own_text = text_f32[pl.ds(start, text_rows), :]
    video = modulated(video_ref[...], vmod_ref[...])
    text = modulated(own_text, tmod_ref[...])
    both = jnp.concatenate([video, text], axis=0).astype(BF16)
    left_ref[...] = both[:, :half]
    right_ref[...] = both[:, half:]


def bands(array, count):
    step = array.shape[-2] // count
    return [array.at[..., i * step : (i + 1) * step, :] for i in range(count)]


def fetch_kernel(counts, *refs):
    many = len(counts)
    copies = []
    for source, landed, count in zip(refs[:many], refs[many : 2 * many], counts):
        for pair in zip(bands(source, count), bands(landed, count)):
            copies.append(pltpu.make_async_copy(*pair, refs[-1].at[len(copies)]))
    for copy in copies:
        copy.start()
    for copy in copies:
        copy.wait()


def head_normed(mixture, gain):
    heads = []
    for h in range(mixture.shape[1] // HD):
        vectors = mixture[:, h * HD : (h + 1) * HD]
        inverse = lax.rsqrt(jnp.mean(vectors * vectors, axis=-1, keepdims=True) + EPS_NORM)
        heads.append(vectors * inverse * gain)
    return jnp.concatenate(heads, axis=1)


def project_kernel(shards, video_rows, *refs):
    chunks = refs[: 2 * shards]
    wv_ref, wt_ref, vgain_ref, tgain_ref, q_ref, kv_ref = refs[2 * shards :]
    width = q_ref.shape[1]
    video, text = [], []
    for side in range(2):
        mine = [chunks[2 * i + side] for i in range(shards)]
        video.append(jnp.concatenate([r[:video_rows, :] for r in mine], axis=0))
        text.append(jnp.concatenate([r[...].astype(F32)[video_rows:] for r in mine], axis=0).astype(BF16))
    half = video[0].shape[1]

    def mixed(sides, w_ref, j):
        total = jnp.dot(sides[0], w_ref[j, :half, :], preferred_element_type=F32)
        return total + jnp.dot(sides[1], w_ref[j, half:, :], preferred_element_type=F32)

    def joined(j, norm):
        v = mixed(video, wv_ref, j)
        t = mixed(text, wt_ref, j)
        if norm:
            v = head_normed(v, vgain_ref[j : j + 1, :])
            t = head_normed(t, tgain_ref[j : j + 1, :])
        return jnp.concatenate([v, t], axis=0).astype(BF16)

    q_ref[...] = joined(0, True)
    kv_ref[:, :width] = joined(1, True)
    kv_ref[:, width:] = joined(2, False)


def wide_rows(refs, counts):
    return jnp.concatenate([r[...].astype(F32)[:n] for r, n in zip(refs, counts)], axis=0).astype(BF16)


def absorbed(state, query, block):
    width = query.shape[1]
    factor = HD ** (-0.5) * math.log2(math.e)
    raised = []
    for h in range(width // HD):
        mine = slice(h * HD, (h + 1) * HD)
        scores = lax.dot_general(
            block[:, mine], query[:, mine], (((1,), (1,)), ((), ())), preferred_element_type=F32
        )
        highest = jnp.max(scores, axis=0, keepdims=True)
        if state:
            before, totals, sums = state[h]
            highest = jnp.maximum(before, highest)
        weights = jnp.exp2((scores - highest) * factor)
        total = jnp.sum(weights, axis=0, keepdims=True)
        mixed = lax.dot_general(
            block[:, width + h * HD : width + (h + 1) * HD],
            weights.astype(BF16),
            (((0,), (0,)), ((), ())),
            preferred_element_type=F32,
        )
        if state:
            shrink = jnp.exp2((before - highest) * factor)
            total = totals * shrink + total
            mixed = sums * shrink + mixed
        raised.append((highest, total, mixed))
    return raised


def load_state(stats_ref, sums_ref):
    heads = stats_ref.shape[0] // 2
    return [
        (
            stats_ref[h : h + 1, :],
            stats_ref[heads + h : heads + h + 1, :],
            sums_ref[h * HD : (h + 1) * HD, :],
        )
        for h in range(heads)
    ]


def absorb_blocks(state, query, blocks, pieces):
    start = 0
    for counts in blocks:
        held = pieces[start : start + len(counts)]
        state = absorbed(state, query, wide_rows(held, counts))
        start += len(counts)
    return state


def attend_kernel(blocks, queries, *refs):
    if queries:
        query = wide_rows(refs[:queries], [r.shape[0] for r in refs[:queries]])
        pieces, (query_ref, stats_ref, sums_ref) = refs[queries:-3], refs[-3:]
        query_ref[...] = query
        state = absorb_blocks([], query, blocks, pieces)
    else:
        query, state = refs[0][...], load_state(*refs[1:3])
        pieces, (stats_ref, sums_ref) = refs[3:-2], refs[-2:]
        state = absorb_blocks(state, query, blocks, pieces)
    heads = len(state)
    for h, (highest, totals, sums) in enumerate(state):
        stats_ref[h : h + 1, :] = highest
        stats_ref[heads + h : heads + h + 1, :] = totals
        sums_ref[h * HD : (h + 1) * HD, :] = sums


def finish_kernel(blocks, sizes, video_rows, query_ref, stats_ref, sums_ref, *refs):
    held = sum(len(counts) for counts in blocks)
    pieces, weights, outs = refs[:held], refs[held : held + 2], refs[held + 2 :]
    state = absorb_blocks(load_state(stats_ref, sums_ref), query_ref[...], blocks, pieces)
    flat = jnp.concatenate([sums / totals for _, totals, sums in state], axis=0)
    rows_out = jnp.transpose(flat)
    text_rows = rows_out.shape[0] // sum(sizes) - video_rows
    video, text = [], []
    start = 0
    for size in sizes:
        video.append(rows_out[start : start + size * video_rows])
        start += size * video_rows
        text.append(rows_out[start : start + size * text_rows])
        start += size * text_rows
    video, text = [jnp.concatenate(rows, axis=0).astype(BF16) for rows in (video, text)]
    video_ref, *outs = outs
    video_ref[...] = video
    lead = outs[0].shape[1]
    left = jnp.dot(video, weights[0][:, :lead], preferred_element_type=F32)
    bands = [
        jnp.dot(text, weights[1][:, c : c + lead], preferred_element_type=F32)
        for c in range(0, weights[1].shape[1], lead)
    ]
    for i, out in enumerate(outs):
        rows = [left[i * video_rows : (i + 1) * video_rows]]
        rows += [y[i * text_rows : (i + 1) * text_rows] for y in bands]
        out[...] = jnp.concatenate(rows, axis=0).astype(BF16)


def right_kernel(video_ref, wv_ref, *outs):
    video_rows, columns = outs[0].shape
    lead = wv_ref.shape[1] - columns
    right = jnp.dot(video_ref[...], wv_ref[:, lead:], preferred_element_type=F32)
    for i, out in enumerate(outs):
        out[...] = right[i * video_rows : (i + 1) * video_rows].astype(BF16)


def close_text_kernel(fa_ref, ba_ref, own_ref, tmod_ref, text_ref):
    text_rows, width = text_ref.shape
    lead = own_ref.shape[1]
    start = own_ref.shape[0] - text_rows * (width // lead)
    total = sum(r[...].astype(F32)[start:] for r in (fa_ref, ba_ref, own_ref))
    for band in range(width // lead):
        columns = slice(band * lead, (band + 1) * lead)
        gate = tmod_ref[2:3, columns].astype(F32)
        text_ref[:, columns] = (total[band * text_rows : (band + 1) * text_rows] * gate).astype(BF16)


def close_kernel(part_ref, fa, ba, own_a, fb, bb, own_b, vmod_ref, *refs):
    pieces, (video_ref, text_ref, wide) = refs[:-3], refs[-3:]
    video_rows, width = video_ref.shape
    lead = own_a.shape[1]
    for columns, arrivals in ((slice(0, lead), (fa, ba, own_a)), (slice(lead, width), (fb, bb, own_b))):
        total = sum(r[...].astype(F32)[:video_rows] for r in arrivals)
        video_ref[:, columns] = (total * vmod_ref[2:3, columns].astype(F32)).astype(BF16)
    rows = pieces[0].shape[0]
    for d, piece in enumerate(pieces):
        start = pl.multiple_of((part_ref[0] ^ d) * rows, rows)
        wide[pl.ds(start, rows), :] = piece[...].astype(F32)
    text_ref[...] = wide[...].astype(BF16)


def local(
    video_tokens,
    text_tokens,
    video_modulation,
    text_modulation,
    video_projection,
    text_projection,
    video_output,
    text_output,
    video_gains,
    text_gains,
):
    n_blk, n_uly = lax.axis_size("blk"), lax.axis_size("uly")
    reach = n_uly // 2
    ahead, back = ring_routes("uly")
    video_rows, width = video_tokens.shape
    half = width // 2
    parts = math.gcd(n_blk, text_tokens.shape[0] // 8)
    text_rows = text_tokens.shape[0] // parts
    shard_rows = video_rows + text_rows
    cols = video_output.shape[0]
    part = lax.rem(lax.axis_index("blk"), parts).reshape(1).astype(jnp.int32)

    chunk = jax.ShapeDtypeStruct((shard_rows, half), BF16)
    own = call(
        modulate_kernel,
        [chunk, chunk],
        (part, video_tokens, text_tokens, video_modulation, text_modulation),
        8,
        [pltpu.VMEM(a.shape, BF16) for a in (video_tokens, text_tokens, video_modulation, text_modulation)]
        + [pltpu.VMEM(text_tokens.shape, F32), pltpu.SemaphoreType.DMA((4,))],
        smem=(0,),
        hbm=(1, 2, 3, 4),
    )

    def fetched(arrays, counts, after):
        arrays = [tied(arrays[0], after), *arrays[1:]]
        return call(
            functools.partial(fetch_kernel, counts),
            [jax.ShapeDtypeStruct(a.shape, a.dtype) for a in arrays],
            arrays,
            1,
            [pltpu.SemaphoreType.DMA((sum(counts),))],
            hbm=range(len(arrays)),
        )

    weights, gains, ends = [], [], []
    waiting = []
    queries, pieces, groups = [], [], []

    def fetch_first(after):
        held = [jnp.transpose(p, (1, 0, 2)) for p in (video_projection, text_projection)]
        *held, vgains, tgains = fetched([*held, video_gains, text_gains], [4, 4, 1, 1], after)
        weights.extend(held)
        gains.extend((vgains, tgains))
        return held[0]

    def fetch_last(after):
        ends.extend(fetched([video_output, text_output], [2, 2], after))
        return ends[0]

    def project(after, direct=False):
        group = list(waiting)
        waiting.clear()
        rows = len(group) * shard_rows
        chunks = [c for _, *pair in group for c in pair]
        q, kv = call(
            functools.partial(project_kernel, len(group), video_rows),
            [
                jax.ShapeDtypeStruct((rows, cols), BF16),
                jax.ShapeDtypeStruct((rows, 2 * cols), BF16),
            ],
            [tied(chunks[0], after), *chunks[1:], *weights, *gains],
            12,
            flops=2 * rows * width * 3 * cols,
        )
        if direct:
            spread = [kv] + [across(kv, d) for d in range(1, n_blk)]
        else:
            spread = {d: across(kv, d) if d else kv for d in (0, 1, *range(2, n_blk, 2))}
        queries.append(q)
        pieces.append(spread)
        groups.append(group)
        return q

    beside = {(1, 1): [fetch_first], (2, 1): [project], (3, 1): [project], (4, 1): [project]}
    fa, fb = own
    ba, bb = own
    waiting.append((0, *own))
    due = []
    for step in range(1, reach + 1):
        behind = fa
        fa = lax.ppermute(tied(fa, *due) if due else fa, "uly", ahead)
        bb = lax.ppermute(bb, "uly", back)
        due = [task(behind) for task in beside.get((step, 0), [])]
        if step < reach:
            behind = fb
            fb = lax.ppermute(tied(fb, *due) if due else fb, "uly", ahead)
            ba = lax.ppermute(ba, "uly", back)
            due = [task(behind) for task in beside.get((step, 1), [])]
            waiting += [(-step, fa, fb), (step, ba, bb)]
        else:
            due = [task(fb) for task in beside.get((step, 1), [])]
            waiting += [(reach, fa, bb)]
            project(fa, True)

    def second_leg(spread, after):
        for d in range(3, n_blk, 2):
            if isinstance(spread, dict):
                spread[d] = across(tied(spread[d - 1], after), 1)

    for spread in pieces[:-1]:
        second_leg(spread, queries[-1])
    sizes = [len(g) for g in groups]
    slots = [r for group in groups for r, *_ in group]
    total_rows = shard_rows * n_uly

    def some(sources, chosen):
        return [
            [
                (pieces[g][d], sizes[g] * (shard_rows if d < parts else video_rows))
                for d in sources[i : i + 2]
                for g in chosen
            ]
            for i in range(0, len(sources), 2)
        ]

    def attended(blocks, given, queries, kernel, outs, extra=(), more=0):
        counts = [[n for _, n in block] for block in blocks]
        keys = [piece for block in blocks for piece, _ in block]
        return call(
            functools.partial(kernel, counts, *queries),
            outs,
            [*given, *keys, *extra],
            16,
            flops=4 * total_rows * sum(map(sum, counts)) * cols + more,
        )

    state = [
        jax.ShapeDtypeStruct((2 * cols // HD, total_rows), F32),
        jax.ShapeDtypeStruct((cols, total_rows), F32),
    ]
    first = range(len(groups) - 1)
    outer = range(2, n_blk)
    query, *carried = attended(
        some((0, 1), first) + some(outer, first[:-1]),
        queries,
        (len(queries),),
        attend_kernel,
        [jax.ShapeDtypeStruct((total_rows, cols), BF16), *state],
    )
    lead = width // 3
    left_rows = video_rows + text_rows * (width // lead)
    shapes = [
        jax.ShapeDtypeStruct((left_rows, lead), BF16),
        jax.ShapeDtypeStruct((video_rows, width - lead), BF16),
    ]
    last = [piece for block in some(outer, first[-1:]) + some(range(n_blk), (len(groups) - 1,)) for piece in block]
    video_heads, *lefts = attended(
        [last],
        [query, *carried],
        (sizes, video_rows),
        finish_kernel,
        [jax.ShapeDtypeStruct((video_rows * n_uly, cols), BF16)] + [shapes[0]] * n_uly,
        (video_output, text_output),
        2 * total_rows * cols * width,
    )
    rights = call(
        right_kernel,
        [shapes[1]] * n_uly,
        [video_heads, video_output],
        16,
        flops=2 * video_rows * n_uly * cols * (width - lead),
    )
    mine = {r: pair for r, *pair in zip(slots, lefts, rights)}
    mine[-reach] = mine[reach]

    def joined(arriving, own_part):
        return (arriving.astype(F32) + own_part.astype(F32)).astype(BF16)

    fa, bb = mine[reach][0], mine[-reach][1]
    fb, ba = mine[reach - 1][1], mine[1 - reach][0]
    for left in range(reach - 1, -1, -1):
        fa = lax.ppermute(fa, "uly", ahead)
        bb = lax.ppermute(bb, "uly", back)
        if left:
            fa = joined(fa, mine[left][0])
            bb = joined(bb, mine[-left][1])
            fb = lax.ppermute(fb, "uly", ahead)
            ba = lax.ppermute(ba, "uly", back)
            if left > 1:
                fb = joined(fb, mine[left - 1][1])
                ba = joined(ba, mine[1 - left][0])
    text_part = call(
        close_text_kernel,
        jax.ShapeDtypeStruct((text_rows, width), BF16),
        (fa, ba, mine[0][0], text_modulation),
        4,
    )
    pieces = [text_part] + [across(text_part, d) for d in range(1, parts)]
    return tuple(
        call(
            close_kernel,
            [jax.ShapeDtypeStruct(t.shape, BF16) for t in (video_tokens, text_tokens)],
            (part, fa, ba, mine[0][0], fb, bb, mine[0][1], video_modulation, *pieces),
            8,
            [pltpu.VMEM(text_tokens.shape, F32)],
            smem=(0,),
        )
    )


def solution(mesh):
    placed = (
        P(("blk", "uly"), None),
        P("uly", None),
        P(),
        P(),
        P(None, None, "uly"),
        P(None, None, "uly"),
        P("uly", None),
        P("uly", None),
        P(),
        P(),
    )
    return jax.shard_map(
        local,
        mesh=mesh,
        in_specs=placed,
        out_specs=(P(("blk", "uly"), None), P("uly", None)),
        check_vma=False,
    )
```
